256 devices in a mesh: det: 16 (over x, z_lo, core), tm: 16 (over z_hi, y).
Axes of the slice: x: 4, y: 4, z: 8 (z_hi: 4, z_lo: 2; z = z_hi * 2 + z_lo), core: 2. Of those that a mesh axis runs over, the one named last changes fastest.
Arguments:
- sky_map: float32 [16384, 128], P('det'), may hold values from -6 to 6
- tile_slot: int32 [256, 24576], P('det', 'tm'), may hold values from 0 to 511
- pixel_offset: int32 [256, 24576], P('det', 'tm'), may hold values from 0 to 127
- tile_list: int32 [16, 16, 16, 32], P('det', 'tm'), may hold values from 0 to 1023, as said below
- noise_kernel: float32 [256, 65], P('det'), may hold values from -0.6 to 0.6
Outputs:
- normal_image: float32 [16384, 128], P('det')
The draws below stay inside these ranges and needn't reach their ends.
Inputs may be any that keep to these rules, and one draw needn't show every extreme that they name: `tile_list`: for each detector group, time span and owner, the 32 entries are distinct tiles of that owner.
All inputs are finite; a program needn't handle non-finite values.
Results may differ from the reference program's by a relative error of at most 0.00007.
Values sent between devices are 32-bit elements; how exact they have to be, the bound alone decides.
A program may use at most 64 MiB of HBM per device.

```python
import math
import jax
import jax.numpy as jnp
import numpy as np
from jax import lax

PIX = 128
W = 64
DET_DEV = 16
T_DEV = 1536
TILE_DEV = 1024
KSLOT = 32
NDET = 256
TIME = 24576
NTILE = 16384
N_DET = 16
N_TM = 16


def draw_tile_list(key, part):
    key = jax.random.fold_in(key, 11)
    row_count = N_DET * N_TM * N_DET
    keys = jax.random.split(key, row_count)
    chosen = jax.vmap(lambda single: jax.random.permutation(single, TILE_DEV)[:KSLOT])(keys)
    return chosen.reshape(N_DET, N_TM, N_DET, KSLOT).astype(jnp.int32)


def place_ends(values, rng, low, high):
    longest = values.shape.index(max(values.shape))
    spots = []
    for shift in (0, 1):
        where = [jax.random.randint(jax.random.fold_in(rng, axis), (), 0, length) for axis, length in enumerate(values.shape)]
        where[longest] = (where[longest] + shift) % values.shape[longest]
        spots.append(tuple(where))
    return values.at[spots[0]].set(low).at[spots[1]].set(high)


def block_levels(stream_key, extent, cuts, least, largest):
    factor_of = 1.0
    for dim, blocks in cuts:
        steps = jax.random.uniform(jax.random.fold_in(jax.random.fold_in(stream_key, 6), dim), (blocks,), jnp.float32, least / len(cuts), largest / len(cuts))
        factor_of = factor_of * jnp.repeat(jnp.exp(steps), extent[dim] // blocks).reshape((-1,) + (1,) * (len(extent) - 1 - dim))
    return factor_of


def cumulative_ranks(count, lean):
    portions = [(1 << 20) // math.isqrt(grade ** lean) + 1 for grade in range(1, count + 1)]
    spread = 1 + sum(portions) // (1 << 30)
    return np.cumsum(np.array([max(1, weight // spread) for weight in portions]))


def ranked(own_key, dims, number_of, skew):
    table = cumulative_ranks(number_of, skew)
    lot = jax.random.randint(jax.random.fold_in(own_key, 1), dims, 0, int(table[number_of - 1]))
    rank = jnp.searchsorted(jnp.asarray(table, jnp.int32), lot, side="right")
    return jax.random.permutation(jax.random.fold_in(own_key, 2), number_of)[rank].astype(jnp.int32)


def normal_values(stream_key, shape, spread, most, cuts=(), kind=jnp.bfloat16):
    loudness = block_levels(stream_key, shape, cuts, -0.22, 0.18) if cuts else 1.0
    entries = jax.random.normal(stream_key, shape, jnp.float32) * spread * loudness
    return jnp.minimum(jnp.maximum(entries, -most), most).astype(kind)


def setup_inputs(seed: int = 0) -> dict:
    key_of = jax.random.split(jax.random.key(seed), 6)
    return {
        "sky_map": normal_values(key_of[0], (NTILE, PIX), 1.0, 6.0, ((0, 16),), jnp.float32),
        "tile_slot": place_ends(ranked(key_of[1], (NDET, TIME), N_DET * KSLOT, 2), jax.random.fold_in(key_of[1], 3), 0, (N_DET * KSLOT) - 1).astype(jnp.int32),
        "pixel_offset": place_ends(jax.random.randint(key_of[2], (NDET, TIME), 0, PIX), jax.random.fold_in(key_of[2], 1), 0, PIX - 1).astype(jnp.int32),
        "tile_list": draw_tile_list(jax.random.fold_in(key_of[5], 71), 0),
        "noise_kernel": normal_values(key_of[4], (NDET, W + 1), 0.12, 0.6, ((0, 16),), jnp.float32),
    }


def filter_rows(padded, noise_kernel):
    row_count, width = padded.shape
    length = width - 2 * W
    blocks = length // PIX
    pieces = (PIX + 2 * W) // PIX
    windows = jnp.stack([padded[:, number * PIX:number * PIX + length].reshape(row_count, blocks, PIX) for number in range(pieces)], axis=2)
    windows = windows.reshape(row_count, blocks, pieces * PIX)
    lag_table = jnp.arange(PIX + 2 * W, dtype=jnp.int32)[:, None] - W - jnp.arange(PIX, dtype=jnp.int32)[None, :]
    distance = jnp.abs(lag_table)
    toeplitz = jnp.where(distance <= W, jnp.take(noise_kernel, jnp.minimum(distance, W), axis=1), jnp.zeros((), jnp.float32))
    result = jnp.einsum("rbm,rmj->rbj", windows, toeplitz, precision=lax.Precision.HIGHEST)
    return result.reshape(row_count, length)


def blocked_filter(padded, noise_kernel):
    row_count, width = padded.shape
    group = 32 if row_count % 32 == 0 else 8
    grouped = padded.reshape(row_count // group, group, width)
    kernels = noise_kernel.reshape(row_count // group, group, W + 1)
    result = lax.map(lambda pair: filter_rows(pair[0], pair[1]), (grouped, kernels))
    return result.reshape(row_count, width - 2 * W)


def reference(sky_map, tile_slot, pixel_offset, tile_list, noise_kernel):
    det_rows, time_len = tile_slot.shape
    owner_base = (jnp.arange(N_DET, dtype=jnp.int32) * TILE_DEV)[None, None, :, None]
    global_list = (tile_list + owner_base).reshape(N_DET, N_TM, N_DET * KSLOT)
    group_rows = (jnp.arange(det_rows, dtype=jnp.int32) // DET_DEV)[:, None]
    span_cols = (jnp.arange(time_len, dtype=jnp.int32) // T_DEV)[None, :]
    tiles = global_list[group_rows, span_cols, tile_slot]
    pixel = tiles * PIX + pixel_offset
    samples = jnp.take(sky_map.reshape(-1), pixel)
    padded = jnp.pad(samples, ((0, 0), (W, W)))
    filtered = blocked_filter(padded, noise_kernel)
    summed = jax.ops.segment_sum(filtered.reshape(-1), pixel.reshape(-1), num_segments=NTILE * PIX)
    return summed.reshape(NTILE, PIX)
```

```python
import jax
import jax.numpy as jnp
from jax import lax
from jax.experimental import pallas as pl
from jax.experimental.pallas import tpu as pltpu
from jax.sharding import PartitionSpec as P

PIX = 128
W = 64
N_DET = 16
N_TM = 16
N_Y = 4
N_Z = 4
ROWS = 16
LENGTH = 1536
BLOCKS = LENGTH // PIX
TILES = 1024
SLOTS = 32
SLOT_ALL = N_DET * SLOTS
SUB = TILES // (N_Y * N_Z)
WIDE = ROWS * PIX

F32 = jnp.float32
BF16 = jnp.bfloat16
I32 = jnp.int32
NT = (((1,), (1,)), ((), ()))
MESH = pl.DeviceIdType.MESH


def halves(values):
    high = values.astype(BF16)
    low = (values - high.astype(F32)).astype(BF16)
    return high, low


def iota(shape, dim):
    return lax.broadcasted_iota(I32, shape, dim)


def one_hot(mask):
    return jnp.where(mask, 1.0, 0.0).astype(BF16)


def build_toeplitz(noise, toeplitz):
    width = 2 * PIX
    place = iota((PIX, width), 1)
    lag = iota((PIX, width), 0)
    pick = one_hot((jnp.abs(place - W) == lag) & (lag <= W))
    coeffs = jnp.concatenate([noise[...], jnp.zeros((ROWS, PIX - W - 1), F32)], axis=1)
    first, rest = halves(coeffs)
    spread = jnp.dot(first, pick, preferred_element_type=F32) + jnp.dot(rest, pick, preferred_element_type=F32)
    for row in range(ROWS):
        wide = jnp.broadcast_to(spread[row : row + 1, :], (PIX, width))
        rolled = pltpu.roll(wide, 0, 1, stride=1, stride_axis=0)
        high, low = halves(rolled)
        toeplitz[row, 0:PIX, :] = high
        toeplitz[row, PIX : 2 * PIX, :] = low


def build_one_hot(slot, selector):
    rank = iota((SLOT_ALL, PIX), 0)

    def step(block, carry):
        span = pl.ds(pl.multiple_of(block * PIX, PIX), PIX)
        for row in range(ROWS):
            selector[block, :, row * PIX : (row + 1) * PIX] = one_hot(rank == slot[row : row + 1, span])
        return carry

    lax.fori_loop(0, BLOCKS, step, 0)


def read_block(block, table, selector, off, store):
    rank = iota((PIX, PIX), 0)
    span = pl.ds(pl.multiple_of(block * PIX, PIX), PIX)
    for row in range(0, ROWS, 2):
        both = jnp.dot(table[...], selector[block, :, row * PIX : (row + 2) * PIX], preferred_element_type=F32)
        both = both[:PIX] + both[PIX:]
        for more in range(2):
            mask = rank == off[row + more : row + more + 1, span]
            part = both[:, more * PIX : (more + 1) * PIX]
            store(row + more, jnp.sum(jnp.where(mask, part, 0.0), axis=0, keepdims=True))


def filter_samples(samples, toeplitz, filtered):
    lane = iota((16, PIX), 1)
    for row in range(ROWS):
        turned = pltpu.roll(samples[row], W, 1)
        window = jnp.where(lane < W, turned, pltpu.roll(turned, 15, 0))
        window = jnp.concatenate([window, pltpu.roll(window, 15, 0)], axis=1)
        high, low = halves(window)
        out = lax.dot_general(jnp.concatenate([high, low], axis=0), toeplitz[row], NT, preferred_element_type=F32)
        filtered[row] = out[:16, :PIX] + out[:16, PIX:] + out[16:, :PIX]


def scatter_samples(filtered, off, selector, spread, total):
    rank = iota((PIX, PIX), 0)
    total[...] = jnp.zeros_like(total)

    def step(block, carry):
        span = pl.ds(pl.multiple_of(block * PIX, PIX), PIX)
        for row in range(ROWS):
            mask = rank == off[row : row + 1, span]
            value = filtered[row, pl.ds(block, 1), :]
            high = value.astype(BF16).astype(F32)
            cols = slice(row * PIX, (row + 1) * PIX)
            spread[0:PIX, cols] = jnp.where(mask, high, 0.0).astype(BF16)
            spread[PIX : 2 * PIX, cols] = jnp.where(mask, value - high, 0.0).astype(BF16)
        total[...] += lax.dot_general(selector[block], spread[...], NT, preferred_element_type=F32)
        return carry

    lax.fori_loop(0, BLOCKS, step, 0)


def kernel(
    sky_h, slot_h, off_h, list_h, noise_h, out_h,
    sky, slot, off, wanted, noise,
    req_out, req_in, rows_out, rows_in, edge_out, edge_in, sums_out, sums_in,
    sky_parts, pick_rows, pick_cols, image, part_y, sum_y, part_z, whole,
    toeplitz, selector, table, samples, filtered, spread, total,
    load_sem, req_s, req_r, rows_s, rows_r, edge_s, edge_r, sums_s, sums_r,
    ry_s, ry_r, rz_s, rz_r, gy_s, gy_r, gz_s, gz_r, save_sem,
):
    group = lax.axis_index("det")
    span = lax.axis_index("tm")
    y = lax.rem(span, N_Y)
    z = lax.div(span, N_Y)

    barrier = pltpu.get_barrier_semaphore()
    for step in range(1, N_DET):
        pl.semaphore_signal(barrier, inc=1, device_id=(lax.rem(group + step, N_DET), span), device_id_type=MESH)
    for step in range(1, N_TM):
        pl.semaphore_signal(barrier, inc=1, device_id=(group, lax.rem(span + step, N_TM)), device_id_type=MESH)

    loads = [
        pltpu.make_async_copy(source, target, load_sem.at[number])
        for number, (source, target) in enumerate(
            [(list_h, wanted), (sky_h, sky), (slot_h, slot), (noise_h, noise), (off_h, off)]
        )
    ]
    for load in loads:
        load.start()

    def remote(source, target, send, recv, device):
        copy = pltpu.make_async_remote_copy(
            src_ref=source, dst_ref=target, send_sem=send, recv_sem=recv, device_id=device, device_id_type=MESH
        )
        copy.start()
        return copy

    sent = []

    loads[0].wait()
    mine = wanted[0, 0]
    mine = jnp.concatenate([mine] * (PIX // SLOTS), axis=1)
    for owner in range(N_DET):
        req_out[owner] = jnp.broadcast_to(mine[owner : owner + 1, :], (8, PIX))
    pl.semaphore_wait(barrier, N_DET + N_TM - 2)
    requests = []
    for step in range(1, N_DET):
        owner = lax.rem(group + step, N_DET)
        requests.append(remote(req_out.at[owner], req_in.at[group], req_s.at[step], req_r.at[step], (owner, span)))
    req_in[group] = req_out[group]

    loads[1].wait()
    high, low = halves(sky[...])
    sky_parts[:, 0:PIX] = high
    sky_parts[:, PIX : 2 * PIX] = low
    for request in requests:
        request.wait_recv()

    lane = iota((1, PIX), 1)
    lists = []
    for four in range(4):
        row = req_in[4 * four, 0:1, :]
        for place in range(1, 4):
            row = jnp.where(lane >= place * SLOTS, req_in[4 * four + place, 0:1, :], row)
        lists.append(row)
    upright = jnp.concatenate(lists + [jnp.zeros((4, PIX), I32)], axis=0).T
    for four in range(4):
        chosen = upright[:, four : four + 1] == iota((PIX, TILES), 1)
        pick_rows[four * PIX : (four + 1) * PIX, :] = one_hot(chosen)
    both = jnp.dot(pick_rows[...], sky_parts[...], preferred_element_type=F32)
    rows_out[...] = (both[:, :PIX] + both[:, PIX:]).reshape(N_DET, SLOTS, PIX)
    tiles = []
    for step in range(1, N_DET):
        reader = lax.rem(group + step, N_DET)
        tiles.append(remote(rows_out.at[reader], rows_in.at[group], rows_s.at[step], rows_r.at[step], (reader, span)))
    rows_in[group] = rows_out[group]

    for four in range(4):
        pick_cols[:, four * PIX : (four + 1) * PIX] = one_hot(iota((TILES, PIX), 0) == lists[four])
    loads[2].wait()
    build_one_hot(slot, selector)
    loads[3].wait()
    build_toeplitz(noise, toeplitz)
    loads[4].wait()
    for tile in tiles:
        tile.wait_recv()

    high, low = halves(rows_in[...].reshape(SLOT_ALL, PIX).T)
    table[0:PIX, :] = high
    table[PIX : 2 * PIX, :] = low

    for side, block in ((0, 0), (1, BLOCKS - 1)):

        def keep_edge(row, value):
            samples[row, block + 1 : block + 2, :] = value
            edge_out[side, row : row + 1, :] = value

        read_block(block, table, selector, off, keep_edge)
    after = lax.rem(span + 1, N_TM)
    before = lax.rem(span + N_TM - 1, N_TM)
    edges = [
        remote(edge_out.at[1], edge_in.at[0], edge_s.at[0], edge_r.at[0], (group, after)),
        remote(edge_out.at[0], edge_in.at[1], edge_s.at[1], edge_r.at[1], (group, before)),
    ]

    def read_step(block, carry):
        def keep(row, value):
            samples[row, pl.ds(block + 1, 1), :] = value

        read_block(block, table, selector, off, keep)
        return carry

    lax.fori_loop(1, BLOCKS - 1, read_step, 0)
    for edge in edges:
        edge.wait_recv()
    left = jnp.where(span > 0, edge_in[0], 0.0)
    right = jnp.where(span < N_TM - 1, edge_in[1], 0.0)
    for row in range(ROWS):
        samples[row, 0:1, :] = left[row : row + 1, :]
        samples[row, BLOCKS + 1 : BLOCKS + 2, :] = right[row : row + 1, :]
        samples[row, BLOCKS + 2 : BLOCKS + 4, :] = jnp.zeros((2, PIX), F32)

    filter_samples(samples, toeplitz, filtered)
    scatter_samples(filtered, off, selector, spread, total)
    sums_out[...] = (total[:, :PIX] + total[:, PIX:]).reshape(N_DET, SLOTS, PIX)

    backs = []
    for step in range(1, N_DET):
        owner = lax.rem(group + step, N_DET)
        backs.append(remote(sums_out.at[owner], sums_in.at[group], sums_s.at[step], sums_r.at[step], (owner, span)))
    sums_in[group] = sums_out[group]
    for back in backs:
        back.wait_recv()
    high, low = halves(sums_in[...].reshape(SLOT_ALL, PIX))
    both = jnp.dot(pick_cols[...], jnp.concatenate([high, low], axis=1), preferred_element_type=F32)
    image[...] = (both[:, :PIX] + both[:, PIX:]).reshape(N_Y, N_Z, SUB, PIX)

    turns = (1, 2, 3, 0)
    over_y = {}
    for turn in turns:
        far = lax.rem(z + turn, N_Z)
        for step in range(1, N_Y):
            peer = lax.rem(y + step, N_Y)
            over_y[turn, step] = remote(
                image.at[peer, far], part_y.at[y, far], ry_s.at[turn, step], ry_r.at[turn, step], (group, z * N_Y + peer)
            )
    over_z = {}
    for turn in turns:
        far = lax.rem(z + turn, N_Z)
        value = image[y, far]
        for step in range(1, N_Y):
            over_y[turn, step].wait_recv()
            value = value + part_y[lax.rem(y + N_Y - step, N_Y), far]
        sum_y[far] = value
        if turn:
            over_z[turn] = remote(sum_y.at[far], part_z.at[z], rz_s.at[turn], rz_r.at[turn], (group, far * N_Y + y))
    value = sum_y[z]
    for turn in turns[:3]:
        over_z[turn].wait_recv()
        value = value + part_z[lax.rem(z + N_Z - turn, N_Z)]
    whole[y, z] = value

    back_z = {}
    for turn in turns[:3]:
        far = lax.rem(z + turn, N_Z)
        back_z[turn] = remote(whole.at[y, z], whole.at[y, z], gz_s.at[turn], gz_r.at[turn], (group, far * N_Y + y))
    back_y = {}
    for turn in (0, 1, 2, 3):
        far = lax.rem(z + N_Z - turn, N_Z)
        if turn:
            back_z[turn].wait_recv()
        for step in range(1, N_Y):
            peer = lax.rem(y + step, N_Y)
            back_y[turn, step] = remote(
                whole.at[y, far], whole.at[y, far], gy_s.at[turn, step], gy_r.at[turn, step], (group, z * N_Y + peer)
            )
    for copy in back_y.values():
        copy.wait_recv()
    save = pltpu.make_async_copy(whole, out_h, save_sem)
    save.start()
    sent = requests + tiles + edges + backs
    for copies in (over_y, over_z, back_z, back_y):
        sent += list(copies.values())
    for copy in sent:
        copy.wait_send()
    save.wait()


def on_device(sky_map, tile_slot, pixel_offset, tile_list, noise_kernel):
    anywhere = pl.BlockSpec(memory_space=pl.ANY)
    dma = pltpu.SemaphoreType.DMA
    vmem = pltpu.VMEM
    result = pl.pallas_call(
        kernel,
        out_shape=jax.ShapeDtypeStruct((N_Y, N_Z, SUB, PIX), F32),
        in_specs=[anywhere] * 5,
        out_specs=anywhere,
        scratch_shapes=[
            vmem((TILES, PIX), F32),
            vmem((ROWS, LENGTH), I32),
            vmem((ROWS, LENGTH), I32),
            vmem((1, 1, N_DET, SLOTS), I32),
            vmem((ROWS, W + 1), F32),
            vmem((N_DET, 8, PIX), I32),
            vmem((N_DET, 8, PIX), I32),
            vmem((N_DET, SLOTS, PIX), F32),
            vmem((N_DET, SLOTS, PIX), F32),
            vmem((2, ROWS, PIX), F32),
            vmem((2, ROWS, PIX), F32),
            vmem((N_DET, SLOTS, PIX), F32),
            vmem((N_DET, SLOTS, PIX), F32),
            vmem((TILES, 2 * PIX), BF16),
            vmem((SLOT_ALL, TILES), BF16),
            vmem((TILES, SLOT_ALL), BF16),
            vmem((N_Y, N_Z, SUB, PIX), F32),
            vmem((N_Y, N_Z, SUB, PIX), F32),
            vmem((N_Z, SUB, PIX), F32),
            vmem((N_Z, SUB, PIX), F32),
            vmem((N_Y, N_Z, SUB, PIX), F32),
            vmem((ROWS, 2 * PIX, 2 * PIX), BF16),
            vmem((BLOCKS, SLOT_ALL, WIDE), BF16),
            vmem((2 * PIX, SLOT_ALL), BF16),
            vmem((ROWS, 16, PIX), F32),
            vmem((ROWS, 16, PIX), F32),
            vmem((2 * PIX, WIDE), BF16),
            vmem((SLOT_ALL, 2 * PIX), F32),
            dma((5,)),
            dma((N_DET,)),
            dma((N_DET,)),
            dma((N_DET,)),
            dma((N_DET,)),
            dma((2,)),
            dma((2,)),
            dma((N_DET,)),
            dma((N_DET,)),
            dma((N_Z, N_Y)),
            dma((N_Z, N_Y)),
            dma((N_Z,)),
            dma((N_Z,)),
            dma((N_Z, N_Y)),
            dma((N_Z, N_Y)),
            dma((N_Z,)),
            dma((N_Z,)),
            dma,
        ],
        compiler_params=pltpu.CompilerParams(
            collective_id=0, has_side_effects=True, vmem_limit_bytes=56 * 1024 * 1024
        ),
    )(sky_map, tile_slot, pixel_offset, tile_list, noise_kernel)
    return result.reshape(TILES, PIX)


def solution(mesh):
    return jax.shard_map(
        on_device,
        mesh=mesh,
        in_specs=(
            P("det", None),
            P("det", "tm"),
            P("det", "tm"),
            P("det", "tm", None, None),
            P("det", None),
        ),
        out_specs=P("det", None),
        check_vma=False,
    )
```

```python
import jax
import jax.numpy as jnp
from jax import lax
from jax.experimental import pallas as pl
from jax.experimental.pallas import tpu as pltpu
from jax.sharding import PartitionSpec as P

PIX = 128
W = 64
N_DET = 16
N_TM = 16
N_Y = 4
N_Z = 4
ROWS = 16
LENGTH = 1536
BLOCKS = LENGTH // PIX
TILES = 1024
SLOTS = 32
SLOT_ALL = N_DET * SLOTS
SUB = TILES // (N_Y * N_Z)
WIDE = ROWS * PIX

F32 = jnp.float32
BF16 = jnp.bfloat16
I32 = jnp.int32
NT = (((1,), (1,)), ((), ()))
MESH = pl.DeviceIdType.MESH


def halves(values):
    high = values.astype(BF16)
    low = (values - high.astype(F32)).astype(BF16)
    return high, low


def iota(shape, dim):
    return lax.broadcasted_iota(I32, shape, dim)


def one_hot(mask):
    return jnp.where(mask, 1.0, 0.0).astype(BF16)


def build_toeplitz(noise, toeplitz):
    width = 2 * PIX
    place = iota((PIX, width), 1)
    lag = iota((PIX, width), 0)
    pick = one_hot((jnp.abs(place - W) == lag) & (lag <= W))
    coeffs = jnp.concatenate([noise[...], jnp.zeros((ROWS, PIX - W - 1), F32)], axis=1)
    first, rest = halves(coeffs)
    spread = jnp.dot(first, pick, preferred_element_type=F32) + jnp.dot(rest, pick, preferred_element_type=F32)
    for row in range(ROWS):
        wide = jnp.broadcast_to(spread[row : row + 1, :], (PIX, width))
        rolled = pltpu.roll(wide, 0, 1, stride=1, stride_axis=0)
        high, low = halves(rolled)
        toeplitz[row, 0:PIX, :] = high
        toeplitz[row, PIX : 2 * PIX, :] = low


def build_one_hot(slot, selector, first, last):
    rank = iota((SLOT_ALL, PIX), 0)

    def step(block, carry):
        span = pl.ds(pl.multiple_of(block * PIX, PIX), PIX)
        for row in range(ROWS):
            selector[block, :, row * PIX : (row + 1) * PIX] = one_hot(rank == slot[row : row + 1, span])
        return carry

    lax.fori_loop(first, last, step, 0)


def read_block(block, table, selector, off, store):
    rank = iota((PIX, PIX), 0)
    span = pl.ds(pl.multiple_of(block * PIX, PIX), PIX)
    for row in range(0, ROWS, 4):
        both = jnp.dot(table[...], selector[block, :, row * PIX : (row + 4) * PIX], preferred_element_type=F32)
        both = both[:PIX] + both[PIX:]
        for more in range(4):
            mask = rank == off[row + more : row + more + 1, span]
            part = both[:, more * PIX : (more + 1) * PIX]
            store(row + more, jnp.sum(jnp.where(mask, part, 0.0), axis=0, keepdims=True))


def filter_samples(samples, toeplitz, filtered):
    lane = iota((16, PIX), 1)
    for row in range(ROWS):
        turned = pltpu.roll(samples[row], W, 1)
        window = jnp.where(lane < W, turned, pltpu.roll(turned, 15, 0))
        window = jnp.concatenate([window, pltpu.roll(window, 15, 0)], axis=1)
        high, low = halves(window)
        out = lax.dot_general(jnp.concatenate([high, low], axis=0), toeplitz[row], NT, preferred_element_type=F32)
        filtered[row] = out[:16, :PIX] + out[:16, PIX:] + out[16:, :PIX]


def scatter_samples(filtered, off, selector, total):
    rank = iota((PIX, PIX), 0)
    total[...] = jnp.zeros_like(total)

    def step(block, carry):
        span = pl.ds(pl.multiple_of(block * PIX, PIX), PIX)
        highs, lows = [], []
        for row in range(ROWS):
            mask = rank == off[row : row + 1, span]
            value = filtered[row, pl.ds(block, 1), :]
            high = value.astype(BF16).astype(F32)
            highs.append(jnp.where(mask, high, 0.0).astype(BF16))
            lows.append(jnp.where(mask, value - high, 0.0).astype(BF16))
        spread = jnp.concatenate([jnp.concatenate(highs, axis=1), jnp.concatenate(lows, axis=1)], axis=0)
        total[...] += lax.dot_general(selector[block], spread, NT, preferred_element_type=F32)
        return carry

    lax.fori_loop(0, BLOCKS, step, 0, unroll=4)


def kernel(
    sky_h, slot_h, off_h, list_h, noise_h, whole,
    sky, slot, off, wanted, noise,
    req_out, req_in, rows_out, rows_in, edge_out, edge_in, sums_out, sums_in,
    sky_parts, pick_rows, pick_cols, image, part_y, sum_y, part_z,
    toeplitz, selector, table, samples, filtered, total,
    load_sem, req_s, req_r, rows_s, rows_r, edge_s, edge_r, sums_s, sums_r,
    ry_s, ry_r, rz_s, rz_r, gy_s, gy_r, gz_s, gz_r,
):
    group = lax.axis_index("det")
    span = lax.axis_index("tm")
    y = lax.rem(span, N_Y)
    z = lax.div(span, N_Y)

    barrier = pltpu.get_barrier_semaphore()
    for step in range(1, N_DET):
        pl.semaphore_signal(barrier, inc=1, device_id=(lax.rem(group + step, N_DET), span), device_id_type=MESH)
    for step in range(1, N_TM):
        pl.semaphore_signal(barrier, inc=1, device_id=(group, lax.rem(span + step, N_TM)), device_id_type=MESH)

    loads = [
        pltpu.make_async_copy(source, target, load_sem.at[number])
        for number, (source, target) in enumerate(
            [(list_h, wanted), (sky_h, sky), (slot_h, slot), (noise_h, noise), (off_h, off)]
        )
    ]
    for load in loads:
        load.start()

    def remote(source, target, send, recv, device):
        copy = pltpu.make_async_remote_copy(
            src_ref=source, dst_ref=target, send_sem=send, recv_sem=recv, device_id=device, device_id_type=MESH
        )
        copy.start()
        return copy

    sent = []

    loads[0].wait()
    mine = wanted[0, 0]
    mine = jnp.concatenate([mine] * (PIX // SLOTS), axis=1)
    for owner in range(N_DET):
        req_out[owner] = jnp.broadcast_to(mine[owner : owner + 1, :], (8, PIX))
    pl.semaphore_wait(barrier, N_DET + N_TM - 2)
    requests = []
    for step in range(1, N_DET):
        owner = lax.rem(group + step, N_DET)
        requests.append(remote(req_out.at[owner], req_in.at[group], req_s.at[step], req_r.at[step], (owner, span)))
    req_in[group] = req_out[group]

    loads[1].wait()
    high, low = halves(sky[...])
    sky_parts[:, 0:PIX] = high
    sky_parts[:, PIX : 2 * PIX] = low
    loads[2].wait()
    build_one_hot(slot, selector, 0, BLOCKS // 2)
    for request in requests:
        request.wait_recv()

    lane = iota((1, PIX), 1)
    lists = []
    for four in range(4):
        row = req_in[4 * four, 0:1, :]
        for place in range(1, 4):
            row = jnp.where(lane >= place * SLOTS, req_in[4 * four + place, 0:1, :], row)
        lists.append(row)
    upright = jnp.concatenate(lists + [jnp.zeros((4, PIX), I32)], axis=0).T
    for four in range(4):
        chosen = upright[:, four : four + 1] == iota((PIX, TILES), 1)
        pick_rows[four * PIX : (four + 1) * PIX, :] = one_hot(chosen)
    both = jnp.dot(pick_rows[...], sky_parts[...], preferred_element_type=F32)
    rows_out[...] = (both[:, :PIX] + both[:, PIX:]).reshape(N_DET, SLOTS, PIX)
    tiles = []
    for step in range(1, N_DET):
        reader = lax.rem(group + step, N_DET)
        tiles.append(remote(rows_out.at[reader], rows_in.at[group], rows_s.at[step], rows_r.at[step], (reader, span)))
    rows_in[group] = rows_out[group]

    for four in range(4):
        pick_cols[:, four * PIX : (four + 1) * PIX] = one_hot(iota((TILES, PIX), 0) == lists[four])
    build_one_hot(slot, selector, BLOCKS // 2, BLOCKS)
    loads[3].wait()
    build_toeplitz(noise, toeplitz)
    loads[4].wait()
    for tile in tiles:
        tile.wait_recv()

    high, low = halves(rows_in[...].reshape(SLOT_ALL, PIX).T)
    table[0:PIX, :] = high
    table[PIX : 2 * PIX, :] = low

    for side, block in ((0, 0), (1, BLOCKS - 1)):

        def keep_edge(row, value):
            samples[row, block + 1 : block + 2, :] = value
            edge_out[side, row : row + 1, :] = value

        read_block(block, table, selector, off, keep_edge)
    after = lax.rem(span + 1, N_TM)
    before = lax.rem(span + N_TM - 1, N_TM)
    edges = [
        remote(edge_out.at[1], edge_in.at[0], edge_s.at[0], edge_r.at[0], (group, after)),
        remote(edge_out.at[0], edge_in.at[1], edge_s.at[1], edge_r.at[1], (group, before)),
    ]

    def read_step(block, carry):
        def keep(row, value):
            samples[row, pl.ds(block + 1, 1), :] = value

        read_block(block, table, selector, off, keep)
        return carry

    lax.fori_loop(1, BLOCKS - 1, read_step, 0, unroll=5)
    for edge in edges:
        edge.wait_recv()
    left = jnp.where(span > 0, edge_in[0], 0.0)
    right = jnp.where(span < N_TM - 1, edge_in[1], 0.0)
    for row in range(ROWS):
        samples[row, 0:1, :] = left[row : row + 1, :]
        samples[row, BLOCKS + 1 : BLOCKS + 2, :] = right[row : row + 1, :]
        samples[row, BLOCKS + 2 : BLOCKS + 4, :] = jnp.zeros((2, PIX), F32)

    filter_samples(samples, toeplitz, filtered)
    scatter_samples(filtered, off, selector, total)
    sums_out[...] = (total[:, :PIX] + total[:, PIX:]).reshape(N_DET, SLOTS, PIX)

    backs = []
    for step in range(1, N_DET):
        owner = lax.rem(group + step, N_DET)
        backs.append(remote(sums_out.at[owner], sums_in.at[group], sums_s.at[step], sums_r.at[step], (owner, span)))
    sums_in[group] = sums_out[group]
    for back in backs:
        back.wait_recv()
    high, low = halves(sums_in[...].reshape(SLOT_ALL, PIX))
    both = jnp.dot(pick_cols[...], jnp.concatenate([high, low], axis=1), preferred_element_type=F32)
    image[...] = (both[:, :PIX] + both[:, PIX:]).reshape(N_Y, N_Z, SUB, PIX)

    turns = (1, 2, 3, 0)
    over_y = {}
    for turn in turns:
        far = lax.rem(z + turn, N_Z)
        for step in range(1, N_Y):
            peer = lax.rem(y + step, N_Y)
            over_y[turn, step] = remote(
                image.at[peer, far], part_y.at[y, far], ry_s.at[turn, step], ry_r.at[turn, step], (group, z * N_Y + peer)
            )
    over_z = {}
    for turn in turns:
        far = lax.rem(z + turn, N_Z)
        value = image[y, far]
        for step in range(1, N_Y):
            over_y[turn, step].wait_recv()
            value = value + part_y[lax.rem(y + N_Y - step, N_Y), far]
        sum_y[far] = value
        if turn:
            over_z[turn] = remote(sum_y.at[far], part_z.at[z], rz_s.at[turn], rz_r.at[turn], (group, far * N_Y + y))
    value = sum_y[z]
    for turn in turns[:3]:
        over_z[turn].wait_recv()
        value = value + part_z[lax.rem(z + N_Z - turn, N_Z)]
    whole[y, z] = value

    back_z = {}
    for turn in turns[:3]:
        far = lax.rem(z + turn, N_Z)
        back_z[turn] = remote(whole.at[y, z], whole.at[y, z], gz_s.at[turn], gz_r.at[turn], (group, far * N_Y + y))
    back_y = {}
    for turn in (0, 1, 2, 3):
        far = lax.rem(z + N_Z - turn, N_Z)
        if turn:
            back_z[turn].wait_recv()
        for step in range(1, N_Y):
            peer = lax.rem(y + step, N_Y)
            back_y[turn, step] = remote(
                whole.at[y, far], whole.at[y, far], gy_s.at[turn, step], gy_r.at[turn, step], (group, z * N_Y + peer)
            )
    for copy in back_y.values():
        copy.wait_recv()
    sent = requests + tiles + edges + backs
    for copies in (over_y, over_z, back_z, back_y):
        sent += list(copies.values())
    for copy in sent:
        copy.wait_send()


def on_device(sky_map, tile_slot, pixel_offset, tile_list, noise_kernel):
    far = pl.BlockSpec(memory_space=pltpu.HBM)
    dma = pltpu.SemaphoreType.DMA
    vmem = pltpu.VMEM
    result = pl.pallas_call(
        kernel,
        out_shape=vmem((N_Y, N_Z, SUB, PIX), F32),
        in_specs=[far] * 5,
        out_specs=pl.BlockSpec(memory_space=vmem),
        scratch_shapes=[
            vmem((TILES, PIX), F32),
            vmem((ROWS, LENGTH), I32),
            vmem((ROWS, LENGTH), I32),
            vmem((1, 1, N_DET, SLOTS), I32),
            vmem((ROWS, W + 1), F32),
            vmem((N_DET, 8, PIX), I32),
            vmem((N_DET, 8, PIX), I32),
            vmem((N_DET, SLOTS, PIX), F32),
            vmem((N_DET, SLOTS, PIX), F32),
            vmem((2, ROWS, PIX), F32),
            vmem((2, ROWS, PIX), F32),
            vmem((N_DET, SLOTS, PIX), F32),
            vmem((N_DET, SLOTS, PIX), F32),
            vmem((TILES, 2 * PIX), BF16),
            vmem((SLOT_ALL, TILES), BF16),
            vmem((TILES, SLOT_ALL), BF16),
            vmem((N_Y, N_Z, SUB, PIX), F32),
            vmem((N_Y, N_Z, SUB, PIX), F32),
            vmem((N_Z, SUB, PIX), F32),
            vmem((N_Z, SUB, PIX), F32),
            vmem((ROWS, 2 * PIX, 2 * PIX), BF16),
            vmem((BLOCKS, SLOT_ALL, WIDE), BF16),
            vmem((2 * PIX, SLOT_ALL), BF16),
            vmem((ROWS, 16, PIX), F32),
            vmem((ROWS, 16, PIX), F32),
            vmem((SLOT_ALL, 2 * PIX), F32),
            dma((5,)),
            dma((N_DET,)),
            dma((N_DET,)),
            dma((N_DET,)),
            dma((N_DET,)),
            dma((2,)),
            dma((2,)),
            dma((N_DET,)),
            dma((N_DET,)),
            dma((N_Z, N_Y)),
            dma((N_Z, N_Y)),
            dma((N_Z,)),
            dma((N_Z,)),
            dma((N_Z, N_Y)),
            dma((N_Z, N_Y)),
            dma((N_Z,)),
            dma((N_Z,)),
        ],
        compiler_params=pltpu.CompilerParams(
            collective_id=0, has_side_effects=True, vmem_limit_bytes=56 * 1024 * 1024
        ),
    )(sky_map, tile_slot, pixel_offset, tile_list, noise_kernel)
    return result.reshape(TILES, PIX)


def solution(mesh):
    return jax.shard_map(
        on_device,
        mesh=mesh,
        in_specs=(
            P("det", None),
            P("det", "tm"),
            P("det", "tm"),
            P("det", "tm", None, None),
            P("det", None),
        ),
        out_specs=P("det", None),
        check_vma=False,
    )
```

```python
import jax
import jax.numpy as jnp
from jax import lax
from jax.experimental import pallas as pl
from jax.experimental.pallas import tpu as pltpu
from jax.sharding import PartitionSpec as P

PIX = 128
W = 64
N_DET = 16
N_TM = 16
N_Y = 4
N_Z = 4
ROWS = 16
LENGTH = 1536
BLOCKS = LENGTH // PIX
TILES = 1024
SLOTS = 32
SLOT_ALL = N_DET * SLOTS
SUB = TILES // (N_Y * N_Z)
PART = PIX // N_Y
FAR_FIRST = (8, 9, 7, 10, 6, 11, 5, 12, 4, 13, 3, 14, 2, 15, 1)
WIDE = ROWS * PIX

F32 = jnp.float32
BF16 = jnp.bfloat16
I32 = jnp.int32
NT = (((1,), (1,)), ((), ()))
MESH = pl.DeviceIdType.MESH


def halves(values):
    high = values.astype(BF16)
    low = (values - high.astype(F32)).astype(BF16)
    return high, low


def iota(shape, dim):
    return lax.broadcasted_iota(I32, shape, dim)


def one_hot(mask):
    return jnp.where(mask, 1.0, 0.0).astype(BF16)


def build_toeplitz(noise, toeplitz):
    width = 2 * PIX
    place = iota((PIX, width), 1)
    lag = iota((PIX, width), 0)
    pick = one_hot((jnp.abs(place - W) == lag) & (lag <= W))
    coeffs = jnp.concatenate([noise[...], jnp.zeros((ROWS, PIX - W - 1), F32)], axis=1)
    first, rest = halves(coeffs)
    spread = jnp.dot(first, pick, preferred_element_type=F32) + jnp.dot(rest, pick, preferred_element_type=F32)
    for row in range(ROWS):
        wide = jnp.broadcast_to(spread[row : row + 1, :], (PIX, width))
        rolled = pltpu.roll(wide, 0, 1, stride=1, stride_axis=0)
        high, low = halves(rolled)
        toeplitz[row, 0:PIX, :] = high
        toeplitz[row, PIX : 2 * PIX, :] = low


def build_one_hot(slot, selector, first, last):
    rank = iota((SLOT_ALL, PIX), 0)

    def step(block, carry):
        span = pl.ds(pl.multiple_of(block * PIX, PIX), PIX)
        for row in range(ROWS):
            selector[block, :, row * PIX : (row + 1) * PIX] = one_hot(rank == slot[row : row + 1, span])
        return carry

    lax.fori_loop(first, last, step, 0)


def read_block(block, table, selector, off, store):
    rank = iota((PIX, PIX), 0)
    span = pl.ds(pl.multiple_of(block * PIX, PIX), PIX)
    for row in range(0, ROWS, 4):
        both = jnp.dot(table[...], selector[block, :, row * PIX : (row + 4) * PIX], preferred_element_type=F32)
        both = both[:PIX] + both[PIX:]
        for more in range(4):
            mask = rank == off[row + more : row + more + 1, span]
            part = both[:, more * PIX : (more + 1) * PIX]
            store(row + more, jnp.sum(jnp.where(mask, part, 0.0), axis=0, keepdims=True))


def filter_samples(samples, toeplitz, filtered):
    lane = iota((16, PIX), 1)
    for row in range(ROWS):
        turned = pltpu.roll(samples[row], W, 1)
        window = jnp.where(lane < W, turned, pltpu.roll(turned, 15, 0))
        window = jnp.concatenate([window, pltpu.roll(window, 15, 0)], axis=1)
        high, low = halves(window)
        out = lax.dot_general(jnp.concatenate([high, low], axis=0), toeplitz[row], NT, preferred_element_type=F32)
        filtered[row] = out[:16, :PIX] + out[:16, PIX:] + out[16:, :PIX]


def lane_part():
    return lax.div(iota((1, PIX), 1), PART)


def turn_parts(values, shifts):
    result = None
    for place, (value, shift) in enumerate(zip(values, shifts)):
        shift = shift % N_Y * PART
        moved = pltpu.roll(value, shift, 1) if shift else value
        result = moved if result is None else jnp.where(lane_part() == place, moved, result)
    return result


def scatter_samples(filtered, off, selector, total):
    rank = iota((PIX, PIX), 0)
    total[...] = jnp.zeros_like(total)

    def step(block, carry):
        span = pl.ds(pl.multiple_of(block * PIX, PIX), PIX)
        highs, lows = [], []
        for row in range(ROWS):
            mask = rank == off[row : row + 1, span]
            value = filtered[row, pl.ds(block, 1), :]
            high = value.astype(BF16).astype(F32)
            highs.append(jnp.where(mask, high, 0.0).astype(BF16))
            lows.append(jnp.where(mask, value - high, 0.0).astype(BF16))
        spread = jnp.concatenate([jnp.concatenate(highs, axis=1), jnp.concatenate(lows, axis=1)], axis=0)
        total[...] += lax.dot_general(selector[block], spread, NT, preferred_element_type=F32)
        return carry

    lax.fori_loop(0, BLOCKS, step, 0, unroll=4)


def kernel(
    sky_h, slot_h, off_h, list_h, noise_h, whole,
    sky, slot, off, noise,
    req_in, list_in, pick_in, rows_out, rows_in, edge_out, edge_in, sums_out, sums_in,
    sky_parts, pick_rows, pick_cols, image, part_z, packed,
    toeplitz, selector, table, samples, filtered, total,
    load_sem, req_s, req_r, pick_s, pick_r, rows_s, rows_r, edge_s, edge_r, sums_s, sums_r,
    rz_s, rz_r, gy_s, gy_r, gz_s, gz_r,
):
    group = lax.axis_index("det")
    span = lax.axis_index("tm")
    y = lax.rem(span, N_Y)
    z = lax.div(span, N_Y)

    barrier = pltpu.get_barrier_semaphore()
    for step in range(1, N_DET):
        pl.semaphore_signal(barrier, inc=1, device_id=(lax.rem(group + step, N_DET), span), device_id_type=MESH)
    for step in range(1, N_TM):
        pl.semaphore_signal(barrier, inc=1, device_id=(group, lax.rem(span + step, N_TM)), device_id_type=MESH)

    loads = [
        pltpu.make_async_copy(source, target, load_sem.at[number])
        for number, (source, target) in enumerate([(list_h.at[0, 0], req_in.at[group]), (sky_h, sky), (slot_h, slot), (noise_h, noise), (off_h, off)])
    ]
    for load in loads:
        load.start()

    def remote(source, target, send, recv, device):
        copy = pltpu.make_async_remote_copy(
            src_ref=source, dst_ref=target, send_sem=send, recv_sem=recv, device_id=device, device_id_type=MESH
        )
        copy.start()
        return copy

    pl.semaphore_wait(barrier, N_DET + N_TM - 2)
    requests = []
    for step in FAR_FIRST:
        owner = lax.rem(group + step, N_DET)
        requests.append(remote(list_h.at[0, 0], req_in.at[group], req_s.at[step], req_r.at[step], (owner, span)))

    loads[1].wait()
    high, low = halves(sky[...])
    sky_parts[:, 0:PIX] = high
    sky_parts[:, PIX : 2 * PIX] = low
    loads[2].wait()
    build_one_hot(slot, selector, 0, BLOCKS // 2)
    loads[0].wait()
    for request in requests:
        request.wait_recv()

    for peer in range(N_DET):
        list_in[peer : peer + 1, 0:SLOTS] = req_in[peer, pl.ds(group, 1), :]
    lists = list_in[:, 0:SLOTS]
    lists = jnp.concatenate([lists] * (PIX // SLOTS), axis=1)
    upright = lists.T
    for peer in range(N_DET):
        chosen = upright[0:SLOTS, peer : peer + 1] == iota((SLOTS, TILES), 1)
        pick_rows[peer * SLOTS : (peer + 1) * SLOTS, :] = one_hot(chosen)
    both = jnp.dot(pick_rows[...], sky_parts[...], preferred_element_type=F32)
    rows_out[...] = (both[:, :PIX] + both[:, PIX:]).reshape(N_DET, SLOTS, PIX)
    tiles = []
    for step in FAR_FIRST:
        reader = lax.rem(group + step, N_DET)
        tiles.append(remote(rows_out.at[reader], rows_in.at[group], rows_s.at[step], rows_r.at[step], (reader, span)))
    rows_in[group] = rows_out[group]

    for peer in range(N_DET):
        list_in[peer : peer + 1, :] = pltpu.roll(lists[peer : peer + 1, :], 8 * peer, 1) if peer else lists[0:1, :]
    own_lane = lax.div(iota((N_DET, PIX), 1), 8) == iota((N_DET, PIX), 0)
    for place in range(N_Y):
        turned = pltpu.roll(list_in[...], PIX - 8 * place, 1) if place else list_in[...]
        pick_in[y, place : place + 1, :] = jnp.sum(jnp.where(own_lane, turned, 0), axis=0, keepdims=True)
    pick_in[y, N_Y : 2 * N_Y, :] = jnp.zeros((N_Y, PIX), I32)
    picks = []
    for step in (2, 1, 3):
        peer = lax.rem(y + step, N_Y)
        picks.append(remote(pick_in.at[y], pick_in.at[y], pick_s.at[step], pick_r.at[step], (group, z * N_Y + peer)))

    build_one_hot(slot, selector, BLOCKS // 2, BLOCKS)
    loads[3].wait()
    build_toeplitz(noise, toeplitz)
    loads[4].wait()
    for tile in tiles:
        tile.wait_recv()

    high, low = halves(rows_in[...].reshape(SLOT_ALL, PIX).T)
    table[0:PIX, :] = high
    table[PIX : 2 * PIX, :] = low

    for side, block in ((0, 0), (1, BLOCKS - 1)):

        def keep_edge(row, value):
            samples[row, block + 1 : block + 2, :] = value
            edge_out[side, row : row + 1, :] = value

        read_block(block, table, selector, off, keep_edge)
    after = lax.rem(span + 1, N_TM)
    before = lax.rem(span + N_TM - 1, N_TM)
    edges = [
        remote(edge_out.at[1], edge_in.at[0], edge_s.at[0], edge_r.at[0], (group, after)),
        remote(edge_out.at[0], edge_in.at[1], edge_s.at[1], edge_r.at[1], (group, before)),
    ]

    def read_step(block, carry):
        def keep(row, value):
            samples[row, pl.ds(block + 1, 1), :] = value

        read_block(block, table, selector, off, keep)
        return carry

    lax.fori_loop(1, BLOCKS - 1, read_step, 0, unroll=5)
    for edge in edges:
        edge.wait_recv()
    left = jnp.where(span > 0, edge_in[0], 0.0)
    right = jnp.where(span < N_TM - 1, edge_in[1], 0.0)
    for row in range(ROWS):
        samples[row, 0:1, :] = left[row : row + 1, :]
        samples[row, BLOCKS + 1 : BLOCKS + 2, :] = right[row : row + 1, :]
        samples[row, BLOCKS + 2 : BLOCKS + 4, :] = jnp.zeros((2, PIX), F32)

    filter_samples(samples, toeplitz, filtered)
    scatter_samples(filtered, off, selector, total)
    sums = (total[:, :PIX] + total[:, PIX:]).reshape(N_DET, N_Y, 8, PIX)
    places = [sums[:, place].reshape(N_DET * 8, PIX) for place in range(N_Y)]
    for part in range(N_Y):
        sums_out[part] = turn_parts(places, [place - part for place in range(N_Y)]).reshape(N_DET, 8, PIX)

    for pick in picks:
        pick.wait_recv()
    backs = []
    for step in FAR_FIRST + (0,):
        owner = lax.rem(group + step, N_DET)
        for more in (2, 1, 3, 0):
            if step or more:
                part = lax.rem(y + more, N_Y)
                backs.append(
                    remote(
                        sums_out.at[part, owner], sums_in.at[y, group],
                        sums_s.at[more, step], sums_r.at[more, step], (owner, z * N_Y + part),
                    )
                )
    sums_in[y, group] = sums_out[y, group]
    for place in range(N_Y):
        for peer in range(N_Y):
            start = (place * N_Y + peer) * PIX
            pick_cols[:, start : start + PIX] = one_hot(iota((TILES, PIX), 0) == pick_in[peer, place : place + 1, :])
    for back in backs:
        back.wait_recv()
    came = sums_in[...].reshape(N_Y * N_DET * 8, PIX)
    came = jnp.concatenate([jnp.where(lane_part() == place, came, 0.0) for place in range(N_Y)], axis=0)
    high, low = halves(came)
    both = jnp.dot(pick_cols[...], jnp.concatenate([high, low], axis=1), preferred_element_type=F32)
    both = both[:, :PIX] + both[:, PIX:]
    both = both + pltpu.roll(both, 2 * PART, 1)
    both = both + pltpu.roll(both, PART, 1)
    both = both.reshape(N_Z, N_Y, SUB, PIX)
    for far in range(N_Z):
        image[far] = turn_parts([both[far, place] for place in range(N_Y)], [0] * N_Y)

    over_z = {}
    for turn in (2, 1, 3):
        far = lax.rem(z + turn, N_Z)
        over_z[turn] = remote(image.at[far], part_z.at[z], rz_s.at[turn], rz_r.at[turn], (group, far * N_Y + y))
    value = image[z]
    for turn in (1, 3, 2):
        over_z[turn].wait_recv()
        value = value + part_z[lax.rem(z + N_Z - turn, N_Z)]
    packed[y, z] = value

    back_z = {}
    for turn in (2, 1, 3):
        far = lax.rem(z + turn, N_Z)
        back_z[turn] = remote(packed.at[y, z], packed.at[y, z], gz_s.at[turn], gz_r.at[turn], (group, far * N_Y + y))
    back_y = {}
    for turn in (0, 1, 3, 2):
        far = lax.rem(z + N_Z - turn, N_Z)
        if turn:
            back_z[turn].wait_recv()
        for step in (2, 1, 3):
            peer = lax.rem(y + step, N_Y)
            back_y[turn, step] = remote(
                packed.at[y, far], packed.at[y, far], gy_s.at[turn, step], gy_r.at[turn, step], (group, z * N_Y + peer)
            )
    for turn in (0, 1, 3, 2):
        far = lax.rem(z + N_Z - turn, N_Z)
        for step in (1, 3, 2):
            back_y[turn, step].wait_recv()
        parts = [packed[part, far] for part in range(N_Y)]
        for place in range(N_Y):
            whole[far, place] = turn_parts(parts, [part - place for part in range(N_Y)])
    sent = requests + picks + tiles + edges + backs
    for copies in (over_z, back_z, back_y):
        sent += list(copies.values())
    for copy in sent:
        copy.wait_send()


def on_device(sky_map, tile_slot, pixel_offset, tile_list, noise_kernel):
    far = pl.BlockSpec(memory_space=pltpu.HBM)
    dma = pltpu.SemaphoreType.DMA
    vmem = pltpu.VMEM
    result = pl.pallas_call(
        kernel,
        out_shape=vmem((N_Y, N_Z, SUB, PIX), F32),
        in_specs=[far] * 5,
        out_specs=pl.BlockSpec(memory_space=vmem),
        scratch_shapes=[
            vmem((TILES, PIX), F32),
            vmem((ROWS, LENGTH), I32),
            vmem((ROWS, LENGTH), I32),
            vmem((ROWS, W + 1), F32),
            vmem((N_DET, N_DET, SLOTS), I32),
            vmem((N_DET, PIX), I32),
            vmem((N_Y, 8, PIX), I32),
            vmem((N_DET, SLOTS, PIX), F32),
            vmem((N_DET, SLOTS, PIX), F32),
            vmem((2, ROWS, PIX), F32),
            vmem((2, ROWS, PIX), F32),
            vmem((N_Y, N_DET, 8, PIX), F32),
            vmem((N_Y, N_DET, 8, PIX), F32),
            vmem((TILES, 2 * PIX), BF16),
            vmem((SLOT_ALL, TILES), BF16),
            vmem((TILES, N_Y * SLOT_ALL), BF16),
            vmem((N_Z, SUB, PIX), F32),
            vmem((N_Z, SUB, PIX), F32),
            vmem((N_Y, N_Z, SUB, PIX), F32),
            vmem((ROWS, 2 * PIX, 2 * PIX), BF16),
            vmem((BLOCKS, SLOT_ALL, WIDE), BF16),
            vmem((2 * PIX, SLOT_ALL), BF16),
            vmem((ROWS, 16, PIX), F32),
            vmem((ROWS, 16, PIX), F32),
            vmem((SLOT_ALL, 2 * PIX), F32),
            dma((5,)),
            dma((N_DET,)),
            dma((N_DET,)),
            dma((N_Y,)),
            dma((N_Y,)),
            dma((N_DET,)),
            dma((N_DET,)),
            dma((2,)),
            dma((2,)),
            dma((N_Y, N_DET)),
            dma((N_Y, N_DET)),
            dma((N_Z,)),
            dma((N_Z,)),
            dma((N_Z, N_Y)),
            dma((N_Z, N_Y)),
            dma((N_Z,)),
            dma((N_Z,)),
        ],
        compiler_params=pltpu.CompilerParams(
            collective_id=0, has_side_effects=True, vmem_limit_bytes=56 * 1024 * 1024
        ),
    )(sky_map, tile_slot, pixel_offset, tile_list, noise_kernel)
    return result.reshape(TILES, PIX)


def solution(mesh):
    return jax.shard_map(
        on_device,
        mesh=mesh,
        in_specs=(
            P("det", None),
            P("det", "tm"),
            P("det", "tm"),
            P("det", "tm", None, None),
            P("det", None),
        ),
        out_specs=P("det", None),
        check_vma=False,
    )
```

```python
import jax
import jax.numpy as jnp
from jax import lax
from jax.experimental import pallas as pl
from jax.experimental.pallas import tpu as pltpu
from jax.sharding import PartitionSpec as P

PIX = 128
W = 64
N_DET = 16
N_TM = 16
N_Y = 4
N_Z = 4
ROWS = 16
LENGTH = 1536
BLOCKS = LENGTH // PIX
TILES = 1024
SLOTS = 32
SLOT_ALL = N_DET * SLOTS
SUB = TILES // (N_Y * N_Z)
PART = PIX // N_Y
FAR_FIRST = (8, 9, 7, 10, 6, 11, 5, 12, 4, 13, 3, 14, 2, 15, 1)
WIDE = ROWS * PIX

F32 = jnp.float32
BF16 = jnp.bfloat16
I32 = jnp.int32
NT = (((1,), (1,)), ((), ()))
MESH = pl.DeviceIdType.MESH


def halves(values):
    high = values.astype(BF16)
    low = (values - high.astype(F32)).astype(BF16)
    return high, low


def iota(shape, dim):
    return lax.broadcasted_iota(I32, shape, dim)


def one_hot(mask):
    return jnp.where(mask, 1.0, 0.0).astype(BF16)


def build_toeplitz(noise, toeplitz):
    width = 2 * PIX
    place = iota((PIX, width), 1)
    lag = iota((PIX, width), 0)
    pick = one_hot((jnp.abs(place - W) == lag) & (lag <= W))
    coeffs = jnp.concatenate([noise[...], jnp.zeros((ROWS, PIX - W - 1), F32)], axis=1)
    first, rest = halves(coeffs)
    spread = jnp.dot(first, pick, preferred_element_type=F32) + jnp.dot(rest, pick, preferred_element_type=F32)
    for row in range(ROWS):
        wide = jnp.broadcast_to(spread[row : row + 1, :], (PIX, width))
        rolled = pltpu.roll(wide, 0, 1, stride=1, stride_axis=0)
        high, low = halves(rolled)
        toeplitz[row, 0:PIX, :] = high
        toeplitz[row, PIX : 2 * PIX, :] = low


def build_one_hot(slot, selector, first, last):
    rank = iota((SLOT_ALL, PIX), 0)

    def step(block, carry):
        span = pl.ds(pl.multiple_of(block * PIX, PIX), PIX)
        for row in range(ROWS):
            selector[block, :, row * PIX : (row + 1) * PIX] = one_hot(rank == slot[row : row + 1, span])
        return carry

    lax.fori_loop(first, last, step, 0)


def read_block(block, table, selector, off, store):
    rank = iota((PIX, PIX), 0)
    span = pl.ds(pl.multiple_of(block * PIX, PIX), PIX)
    for row in range(0, ROWS, 4):
        both = jnp.dot(table[...], selector[block, :, row * PIX : (row + 4) * PIX], preferred_element_type=F32)
        both = both[:PIX] + both[PIX:]
        for more in range(4):
            mask = rank == off[row + more : row + more + 1, span]
            part = both[:, more * PIX : (more + 1) * PIX]
            store(row + more, jnp.sum(jnp.where(mask, part, 0.0), axis=0, keepdims=True))


def filter_samples(samples, toeplitz, filtered):
    lane = iota((16, PIX), 1)
    for row in range(ROWS):
        turned = pltpu.roll(samples[row], W, 1)
        window = jnp.where(lane < W, turned, pltpu.roll(turned, 15, 0))
        window = jnp.concatenate([window, pltpu.roll(window, 15, 0)], axis=1)
        high, low = halves(window)
        out = lax.dot_general(jnp.concatenate([high, low], axis=0), toeplitz[row], NT, preferred_element_type=F32)
        filtered[row] = out[:16, :PIX] + out[:16, PIX:] + out[16:, :PIX]


def lane_part():
    return lax.div(iota((1, PIX), 1), PART)


def turn_parts(values, shifts):
    result = None
    for place, (value, shift) in enumerate(zip(values, shifts)):
        shift = shift % N_Y * PART
        moved = pltpu.roll(value, shift, 1) if shift else value
        result = moved if result is None else jnp.where(lane_part() == place, moved, result)
    return result


def scatter_samples(filtered, off, selector, total):
    rank = iota((PIX, PIX), 0)
    total[...] = jnp.zeros_like(total)

    def step(block, carry):
        span = pl.ds(pl.multiple_of(block * PIX, PIX), PIX)
        highs, lows = [], []
        for row in range(ROWS):
            mask = rank == off[row : row + 1, span]
            value = filtered[row, pl.ds(block, 1), :]
            high = value.astype(BF16).astype(F32)
            highs.append(jnp.where(mask, high, 0.0).astype(BF16))
            lows.append(jnp.where(mask, value - high, 0.0).astype(BF16))
        spread = jnp.concatenate([jnp.concatenate(highs, axis=1), jnp.concatenate(lows, axis=1)], axis=0)
        total[...] += lax.dot_general(selector[block], spread, NT, preferred_element_type=F32)
        return carry

    lax.fori_loop(0, BLOCKS, step, 0, unroll=4)


def kernel(
    sky_h, slot_h, off_h, list_h, noise_h, whole,
    sky, slot, off, noise,
    req_in, list_in, pick_in, rows_out, rows_in, edge_out, edge_in, sums_out, sums_in,
    sky_parts, pick_rows, pick_cols, image, part_z, packed,
    toeplitz, selector, table, samples, filtered, total,
    load_sem, req_s, req_r, pick_s, pick_r, rows_s, rows_r, edge_s, edge_r, sums_s, sums_r,
    rz_s, rz_r, gz_s, gz_r, gy_s, gy_r,
):
    group = lax.axis_index("det")
    span = lax.axis_index("tm")
    y = lax.rem(span, N_Y)
    z = lax.div(span, N_Y)

    barrier = pltpu.get_barrier_semaphore()
    for step in range(1, N_DET):
        pl.semaphore_signal(barrier, inc=1, device_id=(lax.rem(group + step, N_DET), span), device_id_type=MESH)
    for step in range(1, N_Y):
        pl.semaphore_signal(barrier, inc=1, device_id=(group, z * N_Y + lax.rem(y + step, N_Y)), device_id_type=MESH)
    for step in range(1, N_Z):
        pl.semaphore_signal(barrier, inc=1, device_id=(group, lax.rem(z + step, N_Z) * N_Y + y), device_id_type=MESH)
    after = lax.rem(span + 1, N_TM)
    before = lax.rem(span + N_TM - 1, N_TM)

    @pl.when(y == N_Y - 1)
    def greet_after():
        pl.semaphore_signal(barrier, inc=1, device_id=(group, after), device_id_type=MESH)

    @pl.when(y == 0)
    def greet_before():
        pl.semaphore_signal(barrier, inc=1, device_id=(group, before), device_id_type=MESH)

    greeted = N_DET + N_Y + N_Z - 3 + lax.rem(lax.div(y + 1, 2) + 1, 2)

    loads = [
        pltpu.make_async_copy(source, target, load_sem.at[number])
        for number, (source, target) in enumerate([(list_h.at[0, 0], req_in.at[group]), (sky_h, sky), (slot_h, slot), (noise_h, noise), (off_h, off)])
    ]
    for load in loads:
        load.start()

    def descriptor(source, target, send, recv, device):
        return pltpu.make_async_remote_copy(
            src_ref=source, dst_ref=target, send_sem=send, recv_sem=recv, device_id=device, device_id_type=MESH
        )

    def remote(source, target, send, recv, device):
        descriptor(source, target, send, recv, device).start()

    def came(buffer, recv):
        descriptor(buffer, buffer, recv, recv, (group, span)).wait_recv()

    def left(buffer, send):
        descriptor(buffer, buffer, send, send, (group, span)).wait_send()

    pl.semaphore_wait(barrier, greeted)
    for step in FAR_FIRST:
        owner = lax.rem(group + step, N_DET)
        remote(list_h.at[0, 0], req_in.at[group], req_s, req_r, (owner, span))

    loads[1].wait()
    high, low = halves(sky[...])
    sky_parts[:, 0:PIX] = high
    sky_parts[:, PIX : 2 * PIX] = low
    loads[2].wait()
    build_one_hot(slot, selector, 0, BLOCKS // 2)
    loads[0].wait()
    came(req_in.at[0 : N_DET - 1], req_r)

    for peer in range(N_DET):
        list_in[peer : peer + 1, 0:SLOTS] = req_in[peer, pl.ds(group, 1), :]
    lists = list_in[:, 0:SLOTS]
    lists = jnp.concatenate([lists] * (PIX // SLOTS), axis=1)
    upright = lists.T
    for peer in range(N_DET):
        chosen = upright[0:SLOTS, peer : peer + 1] == iota((SLOTS, TILES), 1)
        pick_rows[peer * SLOTS : (peer + 1) * SLOTS, :] = one_hot(chosen)
    both = jnp.dot(pick_rows[...], sky_parts[...], preferred_element_type=F32)
    rows_out[...] = (both[:, :PIX] + both[:, PIX:]).reshape(N_DET, SLOTS, PIX)
    for step in FAR_FIRST:
        reader = lax.rem(group + step, N_DET)
        remote(rows_out.at[reader], rows_in.at[group], rows_s, rows_r, (reader, span))
    rows_in[group] = rows_out[group]

    for peer in range(N_DET):
        list_in[peer : peer + 1, :] = pltpu.roll(lists[peer : peer + 1, :], 8 * peer, 1) if peer else lists[0:1, :]
    own_lane = lax.div(iota((N_DET, PIX), 1), 8) == iota((N_DET, PIX), 0)
    for place in range(N_Y):
        turned = pltpu.roll(list_in[...], PIX - 8 * place, 1) if place else list_in[...]
        pick_in[y, place : place + 1, :] = jnp.sum(jnp.where(own_lane, turned, 0), axis=0, keepdims=True)
    pick_in[y, N_Y : 2 * N_Y, :] = jnp.zeros((N_Y, PIX), I32)
    for step in (2, 1, 3):
        peer = lax.rem(y + step, N_Y)
        remote(pick_in.at[y], pick_in.at[y], pick_s, pick_r, (group, z * N_Y + peer))

    build_one_hot(slot, selector, BLOCKS // 2, BLOCKS)
    loads[3].wait()
    build_toeplitz(noise, toeplitz)
    loads[4].wait()
    came(rows_in.at[0 : N_DET - 1], rows_r)

    high, low = halves(rows_in[...].reshape(SLOT_ALL, PIX).T)
    table[0:PIX, :] = high
    table[PIX : 2 * PIX, :] = low

    for side, block in ((0, 0), (1, BLOCKS - 1)):

        def keep_edge(row, value):
            samples[row, block + 1 : block + 2, :] = value
            edge_out[side, row : row + 1, :] = value

        read_block(block, table, selector, off, keep_edge)
    remote(edge_out.at[1], edge_in.at[0], edge_s, edge_r, (group, after))
    remote(edge_out.at[0], edge_in.at[1], edge_s, edge_r, (group, before))

    def read_step(block, carry):
        def keep(row, value):
            samples[row, pl.ds(block + 1, 1), :] = value

        read_block(block, table, selector, off, keep)
        return carry

    lax.fori_loop(1, BLOCKS - 1, read_step, 0, unroll=5)
    came(edge_in, edge_r)
    first = jnp.where(span > 0, edge_in[0], 0.0)
    last = jnp.where(span < N_TM - 1, edge_in[1], 0.0)
    for row in range(ROWS):
        samples[row, 0:1, :] = first[row : row + 1, :]
        samples[row, BLOCKS + 1 : BLOCKS + 2, :] = last[row : row + 1, :]
        samples[row, BLOCKS + 2 : BLOCKS + 4, :] = jnp.zeros((2, PIX), F32)

    filter_samples(samples, toeplitz, filtered)
    scatter_samples(filtered, off, selector, total)
    sums = (total[:, :PIX] + total[:, PIX:]).reshape(N_DET, N_Y, 8, PIX)
    places = [sums[:, place].reshape(N_DET * 8, PIX) for place in range(N_Y)]
    for part in range(N_Y):
        turned = turn_parts(places, [place - part for place in range(N_Y)])
        sums_out[part * N_DET : (part + 1) * N_DET] = turned.reshape(N_DET, 8, PIX)

    came(pick_in.at[0 : N_Y - 1], pick_r)
    for step in FAR_FIRST + (0,):
        owner = lax.rem(group + step, N_DET)
        for more in (2, 1, 3, 0):
            if step or more:
                part = lax.rem(y + more, N_Y)
                remote(sums_out.at[part * N_DET + owner], sums_in.at[y * N_DET + group], sums_s, sums_r, (owner, z * N_Y + part))
    sums_in[y * N_DET + group] = sums_out[y * N_DET + group]
    for place in range(N_Y):
        for peer in range(N_Y):
            start = (place * N_Y + peer) * PIX
            pick_cols[:, start : start + PIX] = one_hot(iota((TILES, PIX), 0) == pick_in[peer, place : place + 1, :])
    came(sums_in.at[0 : N_Y * N_DET - 1], sums_r)
    rows = sums_in[...].reshape(N_Y * N_DET * 8, PIX)
    rows = jnp.concatenate([jnp.where(lane_part() == place, rows, 0.0) for place in range(N_Y)], axis=0)
    high, low = halves(rows)
    both = jnp.dot(pick_cols[...], jnp.concatenate([high, low], axis=1), preferred_element_type=F32)
    both = both[:, :PIX] + both[:, PIX:]
    both = both + pltpu.roll(both, 2 * PART, 1)
    both = both + pltpu.roll(both, PART, 1)
    both = both.reshape(N_Z, N_Y, SUB, PIX)
    for far in range(N_Z):
        image[far] = turn_parts([both[far, place] for place in range(N_Y)], [0] * N_Y)

    for turn in (2, 1, 3):
        far = lax.rem(z + turn, N_Z)
        remote(image.at[far], part_z.at[z], rz_s, rz_r, (group, far * N_Y + y))
    came(part_z.at[0 : N_Z - 1], rz_r)
    value = image[z]
    for turn in (1, 3, 2):
        value = value + part_z[lax.rem(z + N_Z - turn, N_Z)]
    packed[y, z] = value

    for turn in (2, 1, 3):
        far = lax.rem(z + turn, N_Z)
        remote(packed.at[y, z], packed.at[y, z], gz_s, gz_r.at[turn], (group, far * N_Y + y))
    for turn in (0, 1, 3, 2):
        far = lax.rem(z + N_Z - turn, N_Z)
        if turn:
            came(packed.at[y, far], gz_r.at[turn])
        for step in (2, 1, 3):
            peer = lax.rem(y + step, N_Y)
            remote(packed.at[y, far], packed.at[y, far], gy_s, gy_r.at[turn], (group, z * N_Y + peer))
    for turn in (0, 1, 3, 2):
        far = lax.rem(z + N_Z - turn, N_Z)
        came(packed.at[0 : N_Y - 1, far], gy_r.at[turn])
        parts = [packed[part, far] for part in range(N_Y)]
        for place in range(N_Y):
            whole[far, place] = turn_parts(parts, [part - place for part in range(N_Y)])
    left(req_in.at[0 : N_DET - 1], req_s)
    left(rows_out.at[0 : N_DET - 1], rows_s)
    left(pick_in.at[0 : N_Y - 1], pick_s)
    left(edge_out, edge_s)
    left(sums_out.at[0 : N_Y * N_DET - 1], sums_s)
    left(image.at[0 : N_Z - 1], rz_s)
    left(packed.at[0, 0 : N_Z - 1], gz_s)
    left(packed.at[0 : N_Y - 1], gy_s)


def on_device(sky_map, tile_slot, pixel_offset, tile_list, noise_kernel):
    far = pl.BlockSpec(memory_space=pltpu.HBM)
    dma = pltpu.SemaphoreType.DMA
    vmem = pltpu.VMEM
    result = pl.pallas_call(
        kernel,
        out_shape=vmem((N_Y, N_Z, SUB, PIX), F32),
        in_specs=[far] * 5,
        out_specs=pl.BlockSpec(memory_space=vmem),
        scratch_shapes=[
            vmem((TILES, PIX), F32),
            vmem((ROWS, LENGTH), I32),
            vmem((ROWS, LENGTH), I32),
            vmem((ROWS, W + 1), F32),
            vmem((N_DET, N_DET, SLOTS), I32),
            vmem((N_DET, PIX), I32),
            vmem((N_Y, 8, PIX), I32),
            vmem((N_DET, SLOTS, PIX), F32),
            vmem((N_DET, SLOTS, PIX), F32),
            vmem((2, ROWS, PIX), F32),
            vmem((2, ROWS, PIX), F32),
            vmem((N_Y * N_DET, 8, PIX), F32),
            vmem((N_Y * N_DET, 8, PIX), F32),
            vmem((TILES, 2 * PIX), BF16),
            vmem((SLOT_ALL, TILES), BF16),
            vmem((TILES, N_Y * SLOT_ALL), BF16),
            vmem((N_Z, SUB, PIX), F32),
            vmem((N_Z, SUB, PIX), F32),
            vmem((N_Y, N_Z, SUB, PIX), F32),
            vmem((ROWS, 2 * PIX, 2 * PIX), BF16),
            vmem((BLOCKS, SLOT_ALL, WIDE), BF16),
            vmem((2 * PIX, SLOT_ALL), BF16),
            vmem((ROWS, 16, PIX), F32),
            vmem((ROWS, 16, PIX), F32),
            vmem((SLOT_ALL, 2 * PIX), F32),
            dma((5,)),
            dma,
            dma,
            dma,
            dma,
            dma,
            dma,
            dma,
            dma,
            dma,
            dma,
            dma,
            dma,
            dma,
            dma((N_Z,)),
            dma,
            dma((N_Z,)),
        ],
        compiler_params=pltpu.CompilerParams(
            collective_id=0, has_side_effects=True, vmem_limit_bytes=56 * 1024 * 1024
        ),
    )(sky_map, tile_slot, pixel_offset, tile_list, noise_kernel)
    return result.reshape(TILES, PIX)


def solution(mesh):
    return jax.shard_map(
        on_device,
        mesh=mesh,
        in_specs=(
            P("det", None),
            P("det", "tm"),
            P("det", "tm"),
            P("det", "tm", None, None),
            P("det", None),
        ),
        out_specs=P("det", None),
        check_vma=False,
    )
```

```python
import jax
import jax.numpy as jnp
from jax import lax
from jax.experimental import pallas as pl
from jax.experimental.pallas import tpu as pltpu
from jax.sharding import PartitionSpec as P

PIX = 128
W = 64
N_DET = 16
N_TM = 16
N_Y = 4
N_Z = 4
ROWS = 16
LENGTH = 1536
BLOCKS = LENGTH // PIX
TILES = 1024
SLOTS = 32
SLOT_ALL = N_DET * SLOTS
SUB = TILES // (N_Y * N_Z)
PART = PIX // N_Y
FAR_FIRST = (8, 9, 7, 10, 6, 11, 5, 12, 4, 13, 3, 14, 2, 15, 1)
WIDE = ROWS * PIX
THIRDS = 3 * PIX
HALF = SLOT_ALL // 2

F32 = jnp.float32
BF16 = jnp.bfloat16
F8 = jnp.float8_e4m3fn
I16 = jnp.int16
I32 = jnp.int32
NT = (((1,), (1,)), ((), ()))
MESH = pl.DeviceIdType.MESH


def halves(values):
    high = values.astype(BF16)
    low = (values - high.astype(F32)).astype(BF16)
    return high, low


def iota(shape, dim):
    return lax.broadcasted_iota(I32, shape, dim)


def thirds(values):
    parts = []
    for number in range(3):
        part = values.astype(F8).astype(F32)
        parts.append(part)
        values = (values - part) * 16.0
    return parts


def from_thirds(first, second, third):
    return first + (second + third * 0.0625) * 0.0625


def scale_of(values):
    most = jnp.max(jnp.max(jnp.abs(values), axis=0, keepdims=True), axis=1, keepdims=True)
    most = jnp.maximum(most, 1e-30)
    return 240.0 / most, most * (1.0 / 240.0)


def one_hot(mask):
    return jnp.where(mask, 1.0, 0.0).astype(BF16)


def repeat_row(row, count, dtype):
    return jnp.concatenate([jnp.broadcast_to(row, (16, PIX)).astype(dtype)] * (count // 16), axis=0)


def one_hot_rows(row, count, dtype):
    mask = iota((count, PIX), 0).astype(I16) == repeat_row(row, count, I16)
    return jnp.where(mask, jnp.ones((count, PIX), BF16), jnp.zeros((count, PIX), BF16)).astype(dtype)


def build_toeplitz(noise, toeplitz):
    width = 2 * PIX
    place = iota((PIX, width), 1)
    lag = iota((PIX, width), 0)
    pick = one_hot((jnp.abs(place - W) == lag) & (lag <= W))
    coeffs = jnp.concatenate([noise[...], jnp.zeros((ROWS, PIX - W - 1), F32)], axis=1)
    first, rest = halves(coeffs)
    spread = jnp.dot(first, pick, preferred_element_type=F32) + jnp.dot(rest, pick, preferred_element_type=F32)
    for row in range(ROWS):
        wide = jnp.broadcast_to(spread[row : row + 1, :], (PIX, width))
        rolled = pltpu.roll(wide, 0, 1, stride=1, stride_axis=0)
        high, low = halves(rolled)
        toeplitz[row, 0:PIX, :] = high
        toeplitz[row, PIX : 2 * PIX, :] = low


def build_one_hot(slot, selector, first, last):
    def step(block, carry):
        span = pl.ds(pl.multiple_of(block * PIX, PIX), PIX)
        for row in range(ROWS):
            selector[block, :, row * PIX : (row + 1) * PIX] = one_hot_rows(slot[row : row + 1, span], SLOT_ALL, F8)
        return carry

    lax.fori_loop(first, last, step, 0)


def read_block(block, table, scale, selector, off, store):
    rank = iota((PIX, PIX), 0)
    span = pl.ds(pl.multiple_of(block * PIX, PIX), PIX)
    for row in range(0, ROWS, 4):
        both = jnp.dot(table[...], selector[block, :, row * PIX : (row + 4) * PIX], preferred_element_type=F32)
        both = from_thirds(both[:PIX], both[PIX : 2 * PIX], both[2 * PIX :])
        for more in range(4):
            mask = rank == off[row + more : row + more + 1, span]
            part = both[:, more * PIX : (more + 1) * PIX]
            store(row + more, jnp.sum(jnp.where(mask, part, 0.0), axis=0, keepdims=True) * scale)


def filter_samples(samples, toeplitz, filtered):
    lane = iota((16, PIX), 1)
    for row in range(ROWS):
        turned = pltpu.roll(samples[row], W, 1)
        window = jnp.where(lane < W, turned, pltpu.roll(turned, 15, 0))
        window = jnp.concatenate([window, pltpu.roll(window, 15, 0)], axis=1)
        high, low = halves(window)
        out = lax.dot_general(jnp.concatenate([high, low], axis=0), toeplitz[row], NT, preferred_element_type=F32)
        filtered[row] = out[:16, :PIX] + out[:16, PIX:] + out[16:, :PIX]


def lane_part():
    return lax.div(iota((1, PIX), 1), PART)


def turn_parts(values, shifts):
    result = None
    for place, (value, shift) in enumerate(zip(values, shifts)):
        shift = shift % N_Y * PART
        moved = pltpu.roll(value, shift, 1) if shift else value
        result = moved if result is None else jnp.where(lane_part() == place, moved, result)
    return result


def spread_block(block, parts, off):
    span = pl.ds(pl.multiple_of(block * PIX, PIX), PIX)
    rank = iota((PIX, PIX), 0).astype(I16)
    zeros = jnp.zeros((PIX, PIX), BF16)
    rows = [[], []]
    for row in range(ROWS):
        mask = rank == repeat_row(off[row : row + 1, span], PIX, I16)
        for number in range(2):
            value = repeat_row(parts[number, row, pl.ds(block, 1), :], PIX, BF16)
            rows[number].append(jnp.where(mask, value, zeros))
    return jnp.concatenate([jnp.concatenate(row, axis=1) for row in rows], axis=0)


def scatter_half(start, selector, parts, off, total):
    total[...] = jnp.zeros_like(total)

    def step(block, carry):
        chosen = selector[block, pl.ds(start, HALF), :].astype(BF16)
        total[...] += lax.dot_general(spread_block(block, parts, off), chosen, NT, preferred_element_type=F32)
        return carry

    lax.fori_loop(0, BLOCKS, step, 0, unroll=4)


def kernel(
    sky_h, slot_h, off_h, list_h, noise_h, whole,
    sky, slot, off, noise,
    req_in, list_in, pick_in, rows_out, rows_in, edge_out, edge_in, sums_out, sums_in,
    sky_parts, pick_rows, pick_cols, image, part_z, packed,
    toeplitz, selector, table, samples, filtered, parts, total,
    load_sem, req_s, req_r, pick_s, pick_r, rows_s, rows_r, edge_s, edge_r, sums_s, sums_r,
    rz_s, rz_r, gz_s, gz_r, gy_s, gy_r,
):
    group = lax.axis_index("det")
    span = lax.axis_index("tm")
    y = lax.rem(span, N_Y)
    z = lax.div(span, N_Y)

    barrier = pltpu.get_barrier_semaphore()
    for step in range(1, N_DET):
        pl.semaphore_signal(barrier, inc=1, device_id=(lax.rem(group + step, N_DET), span), device_id_type=MESH)
    for step in range(1, N_Y):
        pl.semaphore_signal(barrier, inc=1, device_id=(group, z * N_Y + lax.rem(y + step, N_Y)), device_id_type=MESH)
    for step in range(1, N_Z):
        pl.semaphore_signal(barrier, inc=1, device_id=(group, lax.rem(z + step, N_Z) * N_Y + y), device_id_type=MESH)
    after = lax.rem(span + 1, N_TM)
    before = lax.rem(span + N_TM - 1, N_TM)

    @pl.when(y == N_Y - 1)
    def greet_after():
        pl.semaphore_signal(barrier, inc=1, device_id=(group, after), device_id_type=MESH)

    @pl.when(y == 0)
    def greet_before():
        pl.semaphore_signal(barrier, inc=1, device_id=(group, before), device_id_type=MESH)

    greeted = N_DET + N_Y + N_Z - 3 + lax.rem(lax.div(y + 1, 2) + 1, 2)

    loads = [
        pltpu.make_async_copy(source, target, load_sem.at[number])
        for number, (source, target) in enumerate([(list_h.at[0, 0], req_in.at[group]), (sky_h, sky), (slot_h, slot), (noise_h, noise), (off_h, off)])
    ]
    for load in loads:
        load.start()

    def descriptor(source, target, send, recv, device):
        return pltpu.make_async_remote_copy(
            src_ref=source, dst_ref=target, send_sem=send, recv_sem=recv, device_id=device, device_id_type=MESH
        )

    def remote(source, target, send, recv, device):
        descriptor(source, target, send, recv, device).start()

    def came(buffer, recv):
        descriptor(buffer, buffer, recv, recv, (group, span)).wait_recv()

    def left(buffer, send):
        descriptor(buffer, buffer, send, send, (group, span)).wait_send()

    pl.semaphore_wait(barrier, greeted)
    for step in FAR_FIRST:
        owner = lax.rem(group + step, N_DET)
        remote(list_h.at[0, 0], req_in.at[group], req_s, req_r, (owner, span))

    loads[1].wait()
    high, low = halves(sky[...])
    sky_parts[:, 0:PIX] = high
    sky_parts[:, PIX : 2 * PIX] = low
    loads[2].wait()
    build_one_hot(slot, selector, 0, BLOCKS // 2)
    loads[0].wait()
    came(req_in.at[0 : N_DET - 1], req_r)

    for peer in range(N_DET):
        list_in[peer : peer + 1, 0:SLOTS] = req_in[peer, pl.ds(group, 1), :]
    lists = list_in[:, 0:SLOTS]
    lists = jnp.concatenate([lists] * (PIX // SLOTS), axis=1)
    upright = lists.T
    for peer in range(N_DET):
        chosen = upright[0:SLOTS, peer : peer + 1] == iota((SLOTS, TILES), 1)
        pick_rows[peer * SLOTS : (peer + 1) * SLOTS, :] = one_hot(chosen)
    both = jnp.dot(pick_rows[...], sky_parts[...], preferred_element_type=F32)
    rows_out[...] = (both[:, :PIX] + both[:, PIX:]).reshape(N_DET, SLOTS, PIX)
    for step in FAR_FIRST:
        reader = lax.rem(group + step, N_DET)
        remote(rows_out.at[reader], rows_in.at[group], rows_s, rows_r, (reader, span))
    rows_in[group] = rows_out[group]

    for peer in range(N_DET):
        list_in[peer : peer + 1, :] = pltpu.roll(lists[peer : peer + 1, :], 8 * peer, 1) if peer else lists[0:1, :]
    own_lane = lax.div(iota((N_DET, PIX), 1), 8) == iota((N_DET, PIX), 0)
    for place in range(N_Y):
        turned = pltpu.roll(list_in[...], PIX - 8 * place, 1) if place else list_in[...]
        pick_in[y, place : place + 1, :] = jnp.sum(jnp.where(own_lane, turned, 0), axis=0, keepdims=True)
    pick_in[y, N_Y : 2 * N_Y, :] = jnp.zeros((N_Y, PIX), I32)
    for step in (2, 1, 3):
        peer = lax.rem(y + step, N_Y)
        remote(pick_in.at[y], pick_in.at[y], pick_s, pick_r, (group, z * N_Y + peer))

    build_one_hot(slot, selector, BLOCKS // 2, BLOCKS)
    loads[3].wait()
    build_toeplitz(noise, toeplitz)
    loads[4].wait()
    came(rows_in.at[0 : N_DET - 1], rows_r)

    values = rows_in[...].reshape(SLOT_ALL, PIX)
    scale, back = scale_of(values)
    for number, part in enumerate(thirds((values * scale).T)):
        table[number * PIX : (number + 1) * PIX, :] = part.astype(F8)

    for side, block in ((0, 0), (1, BLOCKS - 1)):

        def keep_edge(row, value):
            samples[row, block + 1 : block + 2, :] = value
            edge_out[side, row : row + 1, :] = value

        read_block(block, table, back, selector, off, keep_edge)
    remote(edge_out.at[1], edge_in.at[0], edge_s, edge_r, (group, after))
    remote(edge_out.at[0], edge_in.at[1], edge_s, edge_r, (group, before))

    def read_step(block, carry):
        def keep(row, value):
            samples[row, pl.ds(block + 1, 1), :] = value

        read_block(block, table, back, selector, off, keep)
        return carry

    lax.fori_loop(1, BLOCKS - 1, read_step, 0, unroll=5)
    came(edge_in, edge_r)
    first = jnp.where(span > 0, edge_in[0], 0.0)
    last = jnp.where(span < N_TM - 1, edge_in[1], 0.0)
    for row in range(ROWS):
        samples[row, 0:1, :] = first[row : row + 1, :]
        samples[row, BLOCKS + 1 : BLOCKS + 2, :] = last[row : row + 1, :]
        samples[row, BLOCKS + 2 : BLOCKS + 4, :] = jnp.zeros((2, PIX), F32)

    filter_samples(samples, toeplitz, filtered)
    values = filtered[...]
    high = values.astype(BF16).astype(F32)
    parts[0] = high
    parts[1] = values - high

    near = lax.div(group, N_DET // 2)
    for half in (1 - near, near):
        own = half is near
        start = pl.multiple_of(half * HALF, HALF)
        scatter_half(start, selector, parts, off, total)
        sums = (total[:PIX] + total[PIX:]).T.reshape(N_DET // 2, N_Y, 8, PIX)
        places = [sums[:, place].reshape(N_DET * 4, PIX) for place in range(N_Y)]
        for part in range(N_Y):
            turned = turn_parts(places, [place - part for place in range(N_Y)])
            sums_out[pl.ds(part * N_DET + half * (N_DET // 2), N_DET // 2)] = turned.reshape(N_DET // 2, 8, PIX)
        if not own:
            came(pick_in.at[0 : N_Y - 1], pick_r)
        for step in (4, 3, 5, 2, 6, 1, 7, 0):
            owner = half * (N_DET // 2) + lax.rem(group + step, N_DET // 2)
            for more in (2, 1, 3, 0):
                if not own or step or more:
                    part = lax.rem(y + more, N_Y)
                    remote(
                        sums_out.at[part * N_DET + owner], sums_in.at[y * N_DET + group],
                        sums_s, sums_r, (owner, z * N_Y + part),
                    )
    sums_in[y * N_DET + group] = sums_out[y * N_DET + group]
    for peer in range(N_Y):
        for place in range(N_Y):
            chosen = one_hot_rows(pick_in[peer, place : place + 1, :], TILES, BF16)
            start = (peer * N_Y + place) * PIX
            pick_cols[:, start : start + PIX] = chosen
    came(sums_in.at[0 : N_Y * N_DET - 1], sums_r)
    rows = sums_in[...].reshape(N_Y, N_DET * 8, PIX)
    rows = [jnp.where(lane_part() == place, rows[peer], 0.0) for peer in range(N_Y) for place in range(N_Y)]
    high, low = halves(jnp.concatenate(rows, axis=0))
    both = jnp.dot(pick_cols[...], jnp.concatenate([high, low], axis=1), preferred_element_type=F32)
    both = both[:, :PIX] + both[:, PIX:]
    both = both + pltpu.roll(both, 2 * PART, 1)
    both = both + pltpu.roll(both, PART, 1)
    both = both.reshape(N_Z, N_Y, SUB, PIX)
    for far in range(N_Z):
        image[far] = turn_parts([both[far, place] for place in range(N_Y)], [0] * N_Y)

    for turn in (2, 1, 3):
        far = lax.rem(z + turn, N_Z)
        remote(image.at[far], part_z.at[z], rz_s, rz_r, (group, far * N_Y + y))
    came(part_z.at[0 : N_Z - 1], rz_r)
    value = image[z]
    for turn in (1, 3, 2):
        value = value + part_z[lax.rem(z + N_Z - turn, N_Z)]
    packed[y, z] = value

    for turn in (2, 1, 3):
        far = lax.rem(z + turn, N_Z)
        remote(packed.at[y, z], packed.at[y, z], gz_s, gz_r.at[turn], (group, far * N_Y + y))
    for turn in (0, 1, 3, 2):
        far = lax.rem(z + N_Z - turn, N_Z)
        if turn:
            came(packed.at[y, far], gz_r.at[turn])
        for step in (2, 1, 3):
            peer = lax.rem(y + step, N_Y)
            remote(packed.at[y, far], packed.at[y, far], gy_s, gy_r.at[turn], (group, z * N_Y + peer))
    for turn in (0, 1, 3, 2):
        far = lax.rem(z + N_Z - turn, N_Z)
        came(packed.at[0 : N_Y - 1, far], gy_r.at[turn])
        parts = [packed[part, far] for part in range(N_Y)]
        for place in range(N_Y):
            whole[far, place] = turn_parts(parts, [part - place for part in range(N_Y)])
    left(req_in.at[0 : N_DET - 1], req_s)
    left(rows_out.at[0 : N_DET - 1], rows_s)
    left(pick_in.at[0 : N_Y - 1], pick_s)
    left(edge_out, edge_s)
    left(sums_out.at[0 : N_Y * N_DET - 1], sums_s)
    left(image.at[0 : N_Z - 1], rz_s)
    left(packed.at[0, 0 : N_Z - 1], gz_s)
    left(packed.at[0 : N_Y - 1], gy_s)


def on_device(sky_map, tile_slot, pixel_offset, tile_list, noise_kernel):
    far = pl.BlockSpec(memory_space=pltpu.HBM)
    dma = pltpu.SemaphoreType.DMA
    vmem = pltpu.VMEM
    result = pl.pallas_call(
        kernel,
        out_shape=vmem((N_Y, N_Z, SUB, PIX), F32),
        in_specs=[far] * 5,
        out_specs=pl.BlockSpec(memory_space=vmem),
        scratch_shapes=[
            vmem((TILES, PIX), F32),
            vmem((ROWS, LENGTH), I32),
            vmem((ROWS, LENGTH), I32),
            vmem((ROWS, W + 1), F32),
            vmem((N_DET, N_DET, SLOTS), I32),
            vmem((N_DET, PIX), I32),
            vmem((N_Y, 8, PIX), I32),
            vmem((N_DET, SLOTS, PIX), F32),
            vmem((N_DET, SLOTS, PIX), F32),
            vmem((2, ROWS, PIX), F32),
            vmem((2, ROWS, PIX), F32),
            vmem((N_Y * N_DET, 8, PIX), F32),
            vmem((N_Y * N_DET, 8, PIX), F32),
            vmem((TILES, 2 * PIX), BF16),
            vmem((SLOT_ALL, TILES), BF16),
            vmem((TILES, N_Y * SLOT_ALL), BF16),
            vmem((N_Z, SUB, PIX), F32),
            vmem((N_Z, SUB, PIX), F32),
            vmem((N_Y, N_Z, SUB, PIX), F32),
            vmem((ROWS, 2 * PIX, 2 * PIX), BF16),
            vmem((BLOCKS, SLOT_ALL, WIDE), F8),
            vmem((THIRDS, SLOT_ALL), F8),
            vmem((ROWS, 16, PIX), F32),
            vmem((ROWS, 16, PIX), F32),
            vmem((2, ROWS, 16, PIX), F32),
            vmem((2 * PIX, HALF), F32),
            dma((5,)),
            dma,
            dma,
            dma,
            dma,
            dma,
            dma,
            dma,
            dma,
            dma,
            dma,
            dma,
            dma,
            dma,
            dma((N_Z,)),
            dma,
            dma((N_Z,)),
        ],
        compiler_params=pltpu.CompilerParams(
            collective_id=0, has_side_effects=True, vmem_limit_bytes=56 * 1024 * 1024
        ),
    )(sky_map, tile_slot, pixel_offset, tile_list, noise_kernel)
    return result.reshape(TILES, PIX)


def solution(mesh):
    return jax.shard_map(
        on_device,
        mesh=mesh,
        in_specs=(
            P("det", None),
            P("det", "tm"),
            P("det", "tm"),
            P("det", "tm", None, None),
            P("det", None),
        ),
        out_specs=P("det", None),
        check_vma=False,
    )
```

```python
import jax
import jax.numpy as jnp
from jax import lax
from jax.experimental import pallas as pl
from jax.experimental.pallas import tpu as pltpu
from jax.sharding import PartitionSpec as P

PIX = 128
W = 64
N_DET = 16
N_TM = 16
N_Y = 4
N_Z = 4
ROWS = 16
LENGTH = 1536
BLOCKS = LENGTH // PIX
TILES = 1024
SLOTS = 32
SLOT_ALL = N_DET * SLOTS
SUB = TILES // (N_Y * N_Z)
PART = PIX // N_Y
FAR_FIRST = (8, 9, 7, 10, 6, 11, 5, 12, 4, 13, 3, 14, 2, 15, 1)
WIDE = ROWS * PIX
THIRDS = 3 * PIX
HALF = SLOT_ALL // 2

F32 = jnp.float32
BF16 = jnp.bfloat16
F8 = jnp.float8_e4m3fn
I16 = jnp.int16
I32 = jnp.int32
NT = (((1,), (1,)), ((), ()))
MESH = pl.DeviceIdType.MESH


def halves(values):
    high = values.astype(BF16)
    low = (values - high.astype(F32)).astype(BF16)
    return high, low


def iota(shape, dim):
    return lax.broadcasted_iota(I32, shape, dim)


def thirds(values):
    parts = []
    for number in range(3):
        part = values.astype(F8).astype(F32)
        parts.append(part)
        values = (values - part) * 16.0
    return parts


def from_thirds(first, second, third):
    return first + (second + third * 0.0625) * 0.0625


def scale_of(values):
    most = jnp.max(jnp.max(jnp.abs(values), axis=0, keepdims=True), axis=1, keepdims=True)
    most = jnp.maximum(most, 1e-30)
    return 240.0 / most, most * (1.0 / 240.0)


def one_hot(mask):
    return jnp.where(mask, 1.0, 0.0).astype(BF16)


def repeat_row(row, count, dtype):
    return jnp.concatenate([jnp.broadcast_to(row, (16, PIX)).astype(dtype)] * (count // 16), axis=0)


def one_hot_rows(row, count, dtype):
    mask = iota((count, PIX), 0).astype(I16) == repeat_row(row, count, I16)
    return jnp.where(mask, jnp.ones((count, PIX), BF16), jnp.zeros((count, PIX), BF16)).astype(dtype)


def build_toeplitz(noise, toeplitz):
    width = 2 * PIX
    place = iota((PIX, width), 1)
    lag = iota((PIX, width), 0)
    pick = one_hot((jnp.abs(place - W) == lag) & (lag <= W))
    coeffs = jnp.concatenate([noise[...], jnp.zeros((ROWS, PIX - W - 1), F32)], axis=1)
    first, rest = halves(coeffs)
    spread = jnp.dot(first, pick, preferred_element_type=F32) + jnp.dot(rest, pick, preferred_element_type=F32)
    for row in range(ROWS):
        wide = jnp.broadcast_to(spread[row : row + 1, :], (PIX, width))
        rolled = pltpu.roll(wide, 0, 1, stride=1, stride_axis=0)
        high, low = halves(rolled)
        toeplitz[row, 0:PIX, :] = high
        toeplitz[row, PIX : 2 * PIX, :] = low


def build_one_hot(slot, selector, first, last):
    def step(block, carry):
        span = pl.ds(pl.multiple_of(block * PIX, PIX), PIX)
        for row in range(ROWS):
            selector[block, :, row * PIX : (row + 1) * PIX] = one_hot_rows(slot[row : row + 1, span], SLOT_ALL, F8)
        return carry

    lax.fori_loop(first, last, step, 0)


def read_block(block, table, scale, selector, off, store):
    rank = iota((PIX, PIX), 0)
    span = pl.ds(pl.multiple_of(block * PIX, PIX), PIX)
    for row in range(0, ROWS, 8):
        both = jnp.dot(table[...], selector[block, :, row * PIX : (row + 8) * PIX], preferred_element_type=F32)
        both = from_thirds(both[:PIX], both[PIX : 2 * PIX], both[2 * PIX :])
        for more in range(8):
            mask = rank == off[row + more : row + more + 1, span]
            part = both[:, more * PIX : (more + 1) * PIX]
            store(row + more, jnp.sum(jnp.where(mask, part, 0.0), axis=0, keepdims=True) * scale)


def filter_samples(samples, toeplitz, filtered):
    lane = iota((16, PIX), 1)
    for row in range(ROWS):
        turned = pltpu.roll(samples[row], W, 1)
        window = jnp.where(lane < W, turned, pltpu.roll(turned, 15, 0))
        window = jnp.concatenate([window, pltpu.roll(window, 15, 0)], axis=1)
        high, low = halves(window)
        out = lax.dot_general(jnp.concatenate([high, low], axis=0), toeplitz[row], NT, preferred_element_type=F32)
        filtered[row] = out[:16, :PIX] + out[:16, PIX:] + out[16:, :PIX]


def lane_part():
    return lax.div(iota((1, PIX), 1), PART)


def turn_parts(values, shifts):
    result = None
    for place, (value, shift) in enumerate(zip(values, shifts)):
        shift = shift % N_Y * PART
        moved = pltpu.roll(value, shift, 1) if shift else value
        result = moved if result is None else jnp.where(lane_part() == place, moved, result)
    return result


def spread_block(block, parts, off):
    span = pl.ds(pl.multiple_of(block * PIX, PIX), PIX)
    rank = iota((PIX, PIX), 0).astype(I16)
    zeros = jnp.zeros((PIX, PIX), BF16)
    rows = [[], []]
    for row in range(ROWS):
        mask = rank == repeat_row(off[row : row + 1, span], PIX, I16)
        for number in range(2):
            value = repeat_row(parts[number, row, pl.ds(block, 1), :], PIX, BF16)
            rows[number].append(jnp.where(mask, value, zeros))
    return jnp.concatenate([jnp.concatenate(row, axis=1) for row in rows], axis=0)


def scatter_half(start, selector, parts, off, total):
    total[...] = jnp.zeros_like(total)

    def step(block, carry):
        chosen = selector[block, pl.ds(start, HALF), :].astype(BF16)
        total[...] += lax.dot_general(spread_block(block, parts, off), chosen, NT, preferred_element_type=F32)
        return carry

    lax.fori_loop(0, BLOCKS, step, 0, unroll=4)


def kernel(
    sky_h, slot_h, off_h, list_h, noise_h, whole,
    sky, slot, off, noise,
    req_in, list_in, pick_in, rows_out, rows_in, edge_out, edge_in, sums_out, sums_in,
    sky_parts, pick_rows, pick_cols, image, part_z, packed,
    toeplitz, selector, table, samples, filtered, parts, total,
    load_sem, req_s, req_r, pick_s, pick_r, rows_s, rows_r, edge_s, edge_r, sums_s, sums_r,
    rz_s, rz_r, gz_s, gz_r, gy_s, gy_r,
):
    group = lax.axis_index("det")
    span = lax.axis_index("tm")
    y = lax.rem(span, N_Y)
    z = lax.div(span, N_Y)

    barrier = pltpu.get_barrier_semaphore()
    for step in range(1, N_DET):
        pl.semaphore_signal(barrier, inc=1, device_id=(lax.rem(group + step, N_DET), span), device_id_type=MESH)
    for step in range(1, N_Y):
        pl.semaphore_signal(barrier, inc=1, device_id=(group, z * N_Y + lax.rem(y + step, N_Y)), device_id_type=MESH)
    for step in range(1, N_Z):
        pl.semaphore_signal(barrier, inc=1, device_id=(group, lax.rem(z + step, N_Z) * N_Y + y), device_id_type=MESH)
    after = lax.rem(span + 1, N_TM)
    before = lax.rem(span + N_TM - 1, N_TM)

    @pl.when(y == N_Y - 1)
    def greet_after():
        pl.semaphore_signal(barrier, inc=1, device_id=(group, after), device_id_type=MESH)

    @pl.when(y == 0)
    def greet_before():
        pl.semaphore_signal(barrier, inc=1, device_id=(group, before), device_id_type=MESH)

    greeted = N_DET + N_Y + N_Z - 3 + lax.rem(lax.div(y + 1, 2) + 1, 2)

    loads = [
        pltpu.make_async_copy(source, target, load_sem.at[number])
        for number, (source, target) in enumerate([(list_h.at[0, 0], req_in.at[group]), (sky_h, sky), (slot_h, slot), (noise_h, noise), (off_h, off)])
    ]
    for load in loads:
        load.start()

    def descriptor(source, target, send, recv, device):
        return pltpu.make_async_remote_copy(
            src_ref=source, dst_ref=target, send_sem=send, recv_sem=recv, device_id=device, device_id_type=MESH
        )

    def remote(source, target, send, recv, device):
        descriptor(source, target, send, recv, device).start()

    def came(buffer, recv):
        descriptor(buffer, buffer, recv, recv, (group, span)).wait_recv()

    def left(buffer, send):
        descriptor(buffer, buffer, send, send, (group, span)).wait_send()

    pl.semaphore_wait(barrier, greeted)
    for step in FAR_FIRST:
        owner = lax.rem(group + step, N_DET)
        remote(list_h.at[0, 0], req_in.at[group], req_s, req_r, (owner, span))

    loads[1].wait()
    high, low = halves(sky[...])
    sky_parts[:, 0:PIX] = high
    sky_parts[:, PIX : 2 * PIX] = low
    loads[2].wait()
    build_one_hot(slot, selector, 0, BLOCKS // 2)
    loads[0].wait()
    came(req_in.at[0 : N_DET - 1], req_r)

    for peer in range(N_DET):
        list_in[peer : peer + 1, 0:SLOTS] = req_in[peer, pl.ds(group, 1), :]
    lists = list_in[:, 0:SLOTS]
    lists = jnp.concatenate([lists] * (PIX // SLOTS), axis=1)
    upright = lists.T
    for peer in range(N_DET):
        chosen = upright[0:SLOTS, peer : peer + 1] == iota((SLOTS, TILES), 1)
        pick_rows[peer * SLOTS : (peer + 1) * SLOTS, :] = one_hot(chosen)
    both = jnp.dot(pick_rows[...], sky_parts[...], preferred_element_type=F32)
    rows_out[...] = (both[:, :PIX] + both[:, PIX:]).reshape(N_DET, SLOTS, PIX)
    for step in FAR_FIRST:
        reader = lax.rem(group + step, N_DET)
        remote(rows_out.at[reader], rows_in.at[group], rows_s, rows_r, (reader, span))
    rows_in[group] = rows_out[group]

    for peer in range(N_DET):
        list_in[peer : peer + 1, :] = pltpu.roll(lists[peer : peer + 1, :], 8 * peer, 1) if peer else lists[0:1, :]
    own_lane = lax.div(iota((N_DET, PIX), 1), 8) == iota((N_DET, PIX), 0)
    for place in range(N_Y):
        turned = pltpu.roll(list_in[...], PIX - 8 * place, 1) if place else list_in[...]
        pick_in[y, place : place + 1, :] = jnp.sum(jnp.where(own_lane, turned, 0), axis=0, keepdims=True)
    pick_in[y, N_Y : 2 * N_Y, :] = jnp.zeros((N_Y, PIX), I32)
    for step in (2, 1, 3):
        peer = lax.rem(y + step, N_Y)
        remote(pick_in.at[y], pick_in.at[y], pick_s, pick_r, (group, z * N_Y + peer))

    build_one_hot(slot, selector, BLOCKS // 2, BLOCKS)
    loads[3].wait()
    build_toeplitz(noise, toeplitz)
    loads[4].wait()
    came(rows_in.at[0 : N_DET - 1], rows_r)

    values = rows_in[...].reshape(SLOT_ALL, PIX)
    scale, back = scale_of(values)
    for number, part in enumerate(thirds((values * scale).T)):
        table[number * PIX : (number + 1) * PIX, :] = part.astype(F8)

    for side, block in ((0, 0), (1, BLOCKS - 1)):

        def keep_edge(row, value):
            samples[row, block + 1 : block + 2, :] = value
            edge_out[side, row : row + 1, :] = value

        read_block(block, table, back, selector, off, keep_edge)
    remote(edge_out.at[1], edge_in.at[0], edge_s, edge_r, (group, after))
    remote(edge_out.at[0], edge_in.at[1], edge_s, edge_r, (group, before))

    def read_step(block, carry):
        def keep(row, value):
            samples[row, pl.ds(block + 1, 1), :] = value

        read_block(block, table, back, selector, off, keep)
        return carry

    lax.fori_loop(1, BLOCKS - 1, read_step, 0, unroll=5)
    came(edge_in, edge_r)
    first = jnp.where(span > 0, edge_in[0], 0.0)
    last = jnp.where(span < N_TM - 1, edge_in[1], 0.0)
    for row in range(ROWS):
        samples[row, 0:1, :] = first[row : row + 1, :]
        samples[row, BLOCKS + 1 : BLOCKS + 2, :] = last[row : row + 1, :]
        samples[row, BLOCKS + 2 : BLOCKS + 4, :] = jnp.zeros((2, PIX), F32)

    filter_samples(samples, toeplitz, filtered)
    values = filtered[...]
    high = values.astype(BF16).astype(F32)
    parts[0] = high
    parts[1] = values - high

    near = lax.div(group, N_DET // 2)
    for half in (1 - near, near):
        own = half is near
        start = pl.multiple_of(half * HALF, HALF)
        scatter_half(start, selector, parts, off, total)
        sums = (total[:PIX] + total[PIX:]).T.reshape(N_DET // 2, N_Y, 8, PIX)
        places = [sums[:, place].reshape(N_DET * 4, PIX) for place in range(N_Y)]
        for part in range(N_Y):
            turned = turn_parts(places, [place - part for place in range(N_Y)])
            sums_out[pl.ds(part * N_DET + half * (N_DET // 2), N_DET // 2)] = turned.reshape(N_DET // 2, 8, PIX)
        if not own:
            came(pick_in.at[0 : N_Y - 1], pick_r)
        for step in (4, 3, 5, 2, 6, 1, 7, 0):
            owner = half * (N_DET // 2) + lax.rem(group + step, N_DET // 2)
            for more in (2, 1, 3, 0):
                if not own or step or more:
                    part = lax.rem(y + more, N_Y)
                    remote(
                        sums_out.at[part * N_DET + owner], sums_in.at[y * N_DET + group],
                        sums_s, sums_r, (owner, z * N_Y + part),
                    )
    sums_in[y * N_DET + group] = sums_out[y * N_DET + group]
    for peer in range(N_Y):
        for place in range(N_Y):
            chosen = one_hot_rows(pick_in[peer, place : place + 1, :], TILES, BF16)
            start = (peer * N_Y + place) * PIX
            pick_cols[:, start : start + PIX] = chosen
    came(sums_in.at[0 : N_Y * N_DET - 1], sums_r)
    rows = sums_in[...].reshape(N_Y, N_DET * 8, PIX)
    rows = [jnp.where(lane_part() == place, rows[peer], 0.0) for peer in range(N_Y) for place in range(N_Y)]
    high, low = halves(jnp.concatenate(rows, axis=0))
    both = jnp.dot(pick_cols[...], jnp.concatenate([high, low], axis=1), preferred_element_type=F32)
    both = both[:, :PIX] + both[:, PIX:]
    both = both + pltpu.roll(both, 2 * PART, 1)
    both = both + pltpu.roll(both, PART, 1)
    both = both.reshape(N_Z, N_Y, SUB, PIX)
    for far in range(N_Z):
        image[far] = turn_parts([both[far, place] for place in range(N_Y)], [0] * N_Y)

    for turn in (1, 3, 2):
        far = lax.rem(z + turn, N_Z)
        remote(image.at[far], part_z.at[z], rz_s, rz_r, (group, far * N_Y + y))
    came(part_z.at[0 : N_Z - 1], rz_r)
    value = image[z]
    for turn in (1, 3, 2):
        value = value + part_z[lax.rem(z + N_Z - turn, N_Z)]
    packed[y, z] = value

    for turn in (1, 3, 2):
        far = lax.rem(z + turn, N_Z)
        remote(packed.at[y, z], packed.at[y, z], gz_s, gz_r.at[turn], (group, far * N_Y + y))
    for turn in (0, 1, 3, 2):
        far = lax.rem(z + N_Z - turn, N_Z)
        if turn:
            came(packed.at[y, far], gz_r.at[turn])
        for step in (1, 3, 2):
            peer = lax.rem(y + step, N_Y)
            remote(packed.at[y, far], packed.at[y, far], gy_s, gy_r.at[turn], (group, z * N_Y + peer))
    for turn in (0, 1, 3, 2):
        far = lax.rem(z + N_Z - turn, N_Z)
        came(packed.at[0 : N_Y - 1, far], gy_r.at[turn])
        parts = [packed[part, far] for part in range(N_Y)]
        for place in range(N_Y):
            whole[far, place] = turn_parts(parts, [part - place for part in range(N_Y)])
    left(req_in.at[0 : N_DET - 1], req_s)
    left(rows_out.at[0 : N_DET - 1], rows_s)
    left(pick_in.at[0 : N_Y - 1], pick_s)
    left(edge_out, edge_s)
    left(sums_out.at[0 : N_Y * N_DET - 1], sums_s)
    left(image.at[0 : N_Z - 1], rz_s)
    left(packed.at[0, 0 : N_Z - 1], gz_s)
    left(packed.at[0 : N_Y - 1], gy_s)


def on_device(sky_map, tile_slot, pixel_offset, tile_list, noise_kernel):
    far = pl.BlockSpec(memory_space=pltpu.HBM)
    dma = pltpu.SemaphoreType.DMA
    vmem = pltpu.VMEM
    result = pl.pallas_call(
        kernel,
        out_shape=vmem((N_Y, N_Z, SUB, PIX), F32),
        in_specs=[far] * 5,
        out_specs=pl.BlockSpec(memory_space=vmem),
        scratch_shapes=[
            vmem((TILES, PIX), F32),
            vmem((ROWS, LENGTH), I32),
            vmem((ROWS, LENGTH), I32),
            vmem((ROWS, W + 1), F32),
            vmem((N_DET, N_DET, SLOTS), I32),
            vmem((N_DET, PIX), I32),
            vmem((N_Y, 8, PIX), I32),
            vmem((N_DET, SLOTS, PIX), F32),
            vmem((N_DET, SLOTS, PIX), F32),
            vmem((2, ROWS, PIX), F32),
            vmem((2, ROWS, PIX), F32),
            vmem((N_Y * N_DET, 8, PIX), F32),
            vmem((N_Y * N_DET, 8, PIX), F32),
            vmem((TILES, 2 * PIX), BF16),
            vmem((SLOT_ALL, TILES), BF16),
            vmem((TILES, N_Y * SLOT_ALL), BF16),
            vmem((N_Z, SUB, PIX), F32),
            vmem((N_Z, SUB, PIX), F32),
            vmem((N_Y, N_Z, SUB, PIX), F32),
            vmem((ROWS, 2 * PIX, 2 * PIX), BF16),
            vmem((BLOCKS, SLOT_ALL, WIDE), F8),
            vmem((THIRDS, SLOT_ALL), F8),
            vmem((ROWS, 16, PIX), F32),
            vmem((ROWS, 16, PIX), F32),
            vmem((2, ROWS, 16, PIX), F32),
            vmem((2 * PIX, HALF), F32),
            dma((5,)),
            dma,
            dma,
            dma,
            dma,
            dma,
            dma,
            dma,
            dma,
            dma,
            dma,
            dma,
            dma,
            dma,
            dma((N_Z,)),
            dma,
            dma((N_Z,)),
        ],
        compiler_params=pltpu.CompilerParams(
            collective_id=0, has_side_effects=True, vmem_limit_bytes=56 * 1024 * 1024
        ),
    )(sky_map, tile_slot, pixel_offset, tile_list, noise_kernel)
    return result.reshape(TILES, PIX)


def solution(mesh):
    return jax.shard_map(
        on_device,
        mesh=mesh,
        in_specs=(
            P("det", None),
            P("det", "tm"),
            P("det", "tm"),
            P("det", "tm", None, None),
            P("det", None),
        ),
        out_specs=P("det", None),
        check_vma=False,
    )
```

```python
import jax
import jax.numpy as jnp
from jax import lax
from jax.experimental import pallas as pl
from jax.experimental.pallas import tpu as pltpu
from jax.sharding import PartitionSpec as P

PIX = 128
W = 64
N_DET = 16
N_TM = 16
N_Y = 4
N_Z = 4
ROWS = 16
LENGTH = 1536
BLOCKS = LENGTH // PIX
TILES = 1024
SLOTS = 32
SLOT_ALL = N_DET * SLOTS
SUB = TILES // (N_Y * N_Z)
PART = PIX // N_Y
FAR_FIRST = (8, 9, 7, 10, 6, 11, 5, 12, 4, 13, 3, 14, 2, 15, 1)
WIDE = ROWS * PIX
THIRDS = 3 * PIX
HALF = SLOT_ALL // 2

F32 = jnp.float32
BF16 = jnp.bfloat16
F8 = jnp.float8_e4m3fn
I16 = jnp.int16
I32 = jnp.int32
NT = (((1,), (1,)), ((), ()))
MESH = pl.DeviceIdType.MESH


def halves(values):
    high = values.astype(BF16)
    low = (values - high.astype(F32)).astype(BF16)
    return high, low


def iota(shape, dim):
    return lax.broadcasted_iota(I32, shape, dim)


def thirds(values):
    parts = []
    for number in range(3):
        part = values.astype(F8).astype(F32)
        parts.append(part)
        values = (values - part) * 16.0
    return parts


def from_thirds(first, second, third):
    return first + (second + third * 0.0625) * 0.0625


def scale_of(values):
    most = jnp.max(jnp.max(jnp.abs(values), axis=0, keepdims=True), axis=1, keepdims=True)
    most = jnp.maximum(most, 1e-30)
    return 240.0 / most, most * (1.0 / 240.0)


def one_hot(mask):
    return jnp.where(mask, 1.0, 0.0).astype(BF16)


def repeat_row(row, count, dtype):
    return jnp.concatenate([jnp.broadcast_to(row, (16, PIX)).astype(dtype)] * (count // 16), axis=0)


def one_hot_rows(row, count, dtype):
    mask = iota((count, PIX), 0).astype(I16) == repeat_row(row, count, I16)
    return jnp.where(mask, jnp.ones((count, PIX), BF16), jnp.zeros((count, PIX), BF16)).astype(dtype)


def build_toeplitz(noise, toeplitz):
    width = 2 * PIX
    place = iota((PIX, width), 1)
    lag = iota((PIX, width), 0)
    pick = one_hot((jnp.abs(place - W) == lag) & (lag <= W))
    coeffs = jnp.concatenate([noise[...], jnp.zeros((ROWS, PIX - W - 1), F32)], axis=1)
    first, rest = halves(coeffs)
    spread = jnp.dot(first, pick, preferred_element_type=F32) + jnp.dot(rest, pick, preferred_element_type=F32)
    for row in range(ROWS):
        wide = jnp.broadcast_to(spread[row : row + 1, :], (PIX, width))
        rolled = pltpu.roll(wide, 0, 1, stride=1, stride_axis=0)
        high, low = halves(rolled)
        toeplitz[row, 0:PIX, :] = high
        toeplitz[row, PIX : 2 * PIX, :] = low


def build_one_hot(slot, selector, first, last):
    def step(block, carry):
        span = pl.ds(pl.multiple_of(block * PIX, PIX), PIX)
        for row in range(ROWS):
            selector[block, :, row * PIX : (row + 1) * PIX] = one_hot_rows(slot[row : row + 1, span], SLOT_ALL, F8)
        return carry

    lax.fori_loop(first, last, step, 0)


def read_block(block, table, scale, selector, off, store):
    rank = iota((PIX, PIX), 0)
    span = pl.ds(pl.multiple_of(block * PIX, PIX), PIX)
    for row in range(0, ROWS, 8):
        both = jnp.dot(table[...], selector[block, :, row * PIX : (row + 8) * PIX], preferred_element_type=F32)
        both = from_thirds(both[:PIX], both[PIX : 2 * PIX], both[2 * PIX :])
        for more in range(8):
            mask = rank == off[row + more : row + more + 1, span]
            part = both[:, more * PIX : (more + 1) * PIX]
            store(row + more, jnp.sum(jnp.where(mask, part, 0.0), axis=0, keepdims=True) * scale)


def filter_samples(samples, toeplitz, filtered):
    lane = iota((16, PIX), 1)
    for row in range(ROWS):
        turned = pltpu.roll(samples[row], W, 1)
        window = jnp.where(lane < W, turned, pltpu.roll(turned, 15, 0))
        window = jnp.concatenate([window, pltpu.roll(window, 15, 0)], axis=1)
        high, low = halves(window)
        out = lax.dot_general(jnp.concatenate([high, low], axis=0), toeplitz[row], NT, preferred_element_type=F32)
        filtered[row] = out[:16, :PIX] + out[:16, PIX:] + out[16:, :PIX]


def lane_part():
    return lax.div(iota((1, PIX), 1), PART)


def turn_parts(values, shifts):
    result = None
    for place, (value, shift) in enumerate(zip(values, shifts)):
        shift = shift % N_Y * PART
        moved = pltpu.roll(value, shift, 1) if shift else value
        result = moved if result is None else jnp.where(lane_part() == place, moved, result)
    return result


def spread_block(block, parts, off):
    span = pl.ds(pl.multiple_of(block * PIX, PIX), PIX)
    rank = iota((PIX, PIX), 0).astype(I16)
    zeros = jnp.zeros((PIX, PIX), BF16)
    rows = [[], []]
    for row in range(ROWS):
        mask = rank == repeat_row(off[row : row + 1, span], PIX, I16)
        for number in range(2):
            value = repeat_row(parts[number, row, pl.ds(block, 1), :], PIX, BF16)
            rows[number].append(jnp.where(mask, value, zeros))
    return jnp.concatenate([jnp.concatenate(row, axis=1) for row in rows], axis=0)


def scatter_half(start, selector, parts, off, total):
    total[...] = jnp.zeros_like(total)

    def step(block, carry):
        chosen = selector[block, pl.ds(start, HALF), :].astype(BF16)
        total[...] += lax.dot_general(spread_block(block, parts, off), chosen, NT, preferred_element_type=F32)
        return carry

    lax.fori_loop(0, BLOCKS, step, 0, unroll=4)


def kernel(
    sky_h, slot_h, off_h, list_h, noise_h, whole,
    sky, slot, off, noise,
    req_in, list_in, pick_in, rows_out, rows_in, edge_out, edge_in, sums_out, sums_in,
    sky_parts, pick_rows, pick_cols, image, part_z, packed,
    toeplitz, selector, table, samples, filtered, parts, total,
    load_sem, req_s, req_r, pick_s, pick_r, rows_s, rows_r, edge_s, edge_r, sums_s, sums_r,
    rz_s, rz_r, gz_s, gz_r, gy_s, gy_r,
):
    group = lax.axis_index("det")
    span = lax.axis_index("tm")
    y = lax.rem(span, N_Y)
    z = lax.div(span, N_Y)

    barrier = pltpu.get_barrier_semaphore()
    for step in range(1, N_DET):
        pl.semaphore_signal(barrier, inc=1, device_id=(lax.rem(group + step, N_DET), span), device_id_type=MESH)
    for step in range(1, N_Y):
        pl.semaphore_signal(barrier, inc=1, device_id=(group, z * N_Y + lax.rem(y + step, N_Y)), device_id_type=MESH)
    for step in range(1, N_Z):
        pl.semaphore_signal(barrier, inc=1, device_id=(group, lax.rem(z + step, N_Z) * N_Y + y), device_id_type=MESH)
    after = lax.rem(span + 1, N_TM)
    before = lax.rem(span + N_TM - 1, N_TM)

    @pl.when(y == N_Y - 1)
    def greet_after():
        pl.semaphore_signal(barrier, inc=1, device_id=(group, after), device_id_type=MESH)

    @pl.when(y == 0)
    def greet_before():
        pl.semaphore_signal(barrier, inc=1, device_id=(group, before), device_id_type=MESH)

    greeted = N_DET + N_Y + N_Z - 3 + lax.rem(lax.div(y + 1, 2) + 1, 2)

    loads = [
        pltpu.make_async_copy(source, target, load_sem.at[number])
        for number, (source, target) in enumerate([(list_h.at[0, 0], req_in.at[group]), (sky_h, sky), (slot_h, slot), (noise_h, noise), (off_h, off)])
    ]
    for load in loads:
        load.start()

    def descriptor(source, target, send, recv, device):
        return pltpu.make_async_remote_copy(
            src_ref=source, dst_ref=target, send_sem=send, recv_sem=recv, device_id=device, device_id_type=MESH
        )

    def remote(source, target, send, recv, device):
        descriptor(source, target, send, recv, device).start()

    def came(buffer, recv):
        descriptor(buffer, buffer, recv, recv, (group, span)).wait_recv()

    def left(buffer, send):
        descriptor(buffer, buffer, send, send, (group, span)).wait_send()

    pl.semaphore_wait(barrier, greeted)
    for step in FAR_FIRST:
        owner = lax.rem(group + step, N_DET)
        remote(list_h.at[0, 0], req_in.at[group], req_s, req_r, (owner, span))

    loads[1].wait()
    high, low = halves(sky[...])
    sky_parts[:, 0:PIX] = high
    sky_parts[:, PIX : 2 * PIX] = low
    loads[2].wait()
    build_one_hot(slot, selector, 0, BLOCKS // 2)
    loads[0].wait()
    came(req_in.at[0 : N_DET - 1], req_r)

    for peer in range(N_DET):
        list_in[peer : peer + 1, 0:SLOTS] = req_in[peer, pl.ds(group, 1), :]
    lists = list_in[:, 0:SLOTS]
    lists = jnp.concatenate([lists] * (PIX // SLOTS), axis=1)
    upright = lists.T
    for peer in range(N_DET):
        chosen = upright[0:SLOTS, peer : peer + 1] == iota((SLOTS, TILES), 1)
        pick_rows[peer * SLOTS : (peer + 1) * SLOTS, :] = one_hot(chosen)
    both = jnp.dot(pick_rows[...], sky_parts[...], preferred_element_type=F32)
    rows_out[...] = (both[:, :PIX] + both[:, PIX:]).reshape(N_DET, SLOTS, PIX)
    for step in FAR_FIRST:
        reader = lax.rem(group + step, N_DET)
        remote(rows_out.at[reader], rows_in.at[group], rows_s, rows_r, (reader, span))
    rows_in[group] = rows_out[group]

    for peer in range(N_DET):
        list_in[peer : peer + 1, :] = pltpu.roll(lists[peer : peer + 1, :], 8 * peer, 1) if peer else lists[0:1, :]
    own_lane = lax.div(iota((N_DET, PIX), 1), 8) == iota((N_DET, PIX), 0)
    for place in range(N_Y):
        turned = pltpu.roll(list_in[...], PIX - 8 * place, 1) if place else list_in[...]
        pick_in[y, place : place + 1, :] = jnp.sum(jnp.where(own_lane, turned, 0), axis=0, keepdims=True)
    pick_in[y, N_Y : 2 * N_Y, :] = jnp.zeros((N_Y, PIX), I32)
    for step in (2, 1, 3):
        peer = lax.rem(y + step, N_Y)
        remote(pick_in.at[y], pick_in.at[y], pick_s, pick_r, (group, z * N_Y + peer))

    build_one_hot(slot, selector, BLOCKS // 2, BLOCKS)
    loads[3].wait()
    build_toeplitz(noise, toeplitz)
    loads[4].wait()
    came(rows_in.at[0 : N_DET - 1], rows_r)

    values = rows_in[...].reshape(SLOT_ALL, PIX)
    scale, back = scale_of(values)
    for number, part in enumerate(thirds((values * scale).T)):
        table[number * PIX : (number + 1) * PIX, :] = part.astype(F8)

    for side, block in ((0, 0), (1, BLOCKS - 1)):

        def keep_edge(row, value):
            samples[row, block + 1 : block + 2, :] = value
            edge_out[side, row : row + 1, :] = value

        read_block(block, table, back, selector, off, keep_edge)
    remote(edge_out.at[1], edge_in.at[0], edge_s, edge_r, (group, after))
    remote(edge_out.at[0], edge_in.at[1], edge_s, edge_r, (group, before))

    def read_step(block, carry):
        def keep(row, value):
            samples[row, pl.ds(block + 1, 1), :] = value

        read_block(block, table, back, selector, off, keep)
        return carry

    lax.fori_loop(1, BLOCKS - 1, read_step, 0, unroll=5)
    came(edge_in, edge_r)
    first = jnp.where(span > 0, edge_in[0], 0.0)
    last = jnp.where(span < N_TM - 1, edge_in[1], 0.0)
    for row in range(ROWS):
        samples[row, 0:1, :] = first[row : row + 1, :]
        samples[row, BLOCKS + 1 : BLOCKS + 2, :] = last[row : row + 1, :]
        samples[row, BLOCKS + 2 : BLOCKS + 4, :] = jnp.zeros((2, PIX), F32)

    filter_samples(samples, toeplitz, filtered)
    values = filtered[...]
    high = values.astype(BF16).astype(F32)
    parts[0] = high
    parts[1] = values - high

    near = lax.div(group, N_DET // 2)
    for half in (1 - near, near):
        own = half is near
        start = pl.multiple_of(half * HALF, HALF)
        scatter_half(start, selector, parts, off, total)
        sums = (total[:PIX] + total[PIX:]).T.reshape(N_DET // 2, N_Y, 8, PIX)
        places = [sums[:, place].reshape(N_DET * 4, PIX) for place in range(N_Y)]
        for part in range(N_Y):
            turned = turn_parts(places, [place - part for place in range(N_Y)])
            sums_out[pl.ds(part * N_DET + half * (N_DET // 2), N_DET // 2)] = turned.reshape(N_DET // 2, 8, PIX)
        if not own:
            came(pick_in.at[0 : N_Y - 1], pick_r)
        for step in (4, 3, 5, 2, 6, 1, 7, 0):
            owner = half * (N_DET // 2) + lax.rem(group + step, N_DET // 2)
            for more in (2, 1, 3, 0):
                if not own or step or more:
                    part = lax.rem(y + more, N_Y)
                    remote(
                        sums_out.at[part * N_DET + owner], sums_in.at[y * N_DET + group],
                        sums_s, sums_r, (owner, z * N_Y + part),
                    )
    sums_in[y * N_DET + group] = sums_out[y * N_DET + group]
    for peer in range(N_Y):
        for place in range(N_Y):
            chosen = one_hot_rows(pick_in[peer, place : place + 1, :], TILES, BF16)
            start = (peer * N_Y + place) * PIX
            pick_cols[:, start : start + PIX] = chosen
    came(sums_in.at[0 : N_Y * N_DET - 1], sums_r)
    rows = sums_in[...].reshape(N_Y, N_DET * 8, PIX)
    rows = [jnp.where(lane_part() == place, rows[peer], 0.0) for peer in range(N_Y) for place in range(N_Y)]
    high, low = halves(jnp.concatenate(rows, axis=0))
    both = jnp.dot(pick_cols[...], jnp.concatenate([high, low], axis=1), preferred_element_type=F32)
    both = both[:, :PIX] + both[:, PIX:]
    both = both + pltpu.roll(both, 2 * PART, 1)
    both = both + pltpu.roll(both, PART, 1)
    both = both.reshape(N_Z, N_Y, SUB, PIX)
    for far in range(N_Z):
        image[far] = turn_parts([both[far, place] for place in range(N_Y)], [0] * N_Y)

    for turn in (1, 3, 2):
        far = lax.rem(z + turn, N_Z)
        remote(image.at[far], part_z.at[z], rz_s, rz_r, (group, far * N_Y + y))
    left(req_in.at[0 : N_DET - 1], req_s)
    left(rows_out.at[0 : N_DET - 1], rows_s)
    left(pick_in.at[0 : N_Y - 1], pick_s)
    left(edge_out, edge_s)
    left(sums_out.at[0 : N_Y * N_DET - 1], sums_s)
    came(part_z.at[0 : N_Z - 1], rz_r)
    value = image[z]
    for turn in (1, 3, 2):
        value = value + part_z[lax.rem(z + N_Z - turn, N_Z)]
    packed[y, z] = value

    for turn in (1, 3, 2):
        far = lax.rem(z + turn, N_Z)
        remote(packed.at[y, z], packed.at[y, z], gz_s, gz_r.at[turn], (group, far * N_Y + y))
    for turn in (0, 1, 3, 2):
        far = lax.rem(z + N_Z - turn, N_Z)
        if turn == 1:
            left(image.at[0 : N_Z - 1], rz_s)
        if turn:
            came(packed.at[y, far], gz_r.at[turn])
        for step in (1, 3, 2):
            peer = lax.rem(y + step, N_Y)
            remote(packed.at[y, far], packed.at[y, far], gy_s, gy_r.at[turn], (group, z * N_Y + peer))
    for turn in (0, 1, 3, 2):
        far = lax.rem(z + N_Z - turn, N_Z)
        came(packed.at[0 : N_Y - 1, far], gy_r.at[turn])
        parts = [packed[part, far] for part in range(N_Y)]
        for place in range(N_Y):
            whole[far, place] = turn_parts(parts, [part - place for part in range(N_Y)])
    left(packed.at[0, 0 : N_Z - 1], gz_s)
    left(packed.at[0 : N_Y - 1], gy_s)


def on_device(sky_map, tile_slot, pixel_offset, tile_list, noise_kernel):
    far = pl.BlockSpec(memory_space=pltpu.HBM)
    dma = pltpu.SemaphoreType.DMA
    vmem = pltpu.VMEM
    result = pl.pallas_call(
        kernel,
        out_shape=vmem((N_Y, N_Z, SUB, PIX), F32),
        in_specs=[far] * 5,
        out_specs=pl.BlockSpec(memory_space=vmem),
        scratch_shapes=[
            vmem((TILES, PIX), F32),
            vmem((ROWS, LENGTH), I32),
            vmem((ROWS, LENGTH), I32),
            vmem((ROWS, W + 1), F32),
            vmem((N_DET, N_DET, SLOTS), I32),
            vmem((N_DET, PIX), I32),
            vmem((N_Y, 8, PIX), I32),
            vmem((N_DET, SLOTS, PIX), F32),
            vmem((N_DET, SLOTS, PIX), F32),
            vmem((2, ROWS, PIX), F32),
            vmem((2, ROWS, PIX), F32),
            vmem((N_Y * N_DET, 8, PIX), F32),
            vmem((N_Y * N_DET, 8, PIX), F32),
            vmem((TILES, 2 * PIX), BF16),
            vmem((SLOT_ALL, TILES), BF16),
            vmem((TILES, N_Y * SLOT_ALL), BF16),
            vmem((N_Z, SUB, PIX), F32),
            vmem((N_Z, SUB, PIX), F32),
            vmem((N_Y, N_Z, SUB, PIX), F32),
            vmem((ROWS, 2 * PIX, 2 * PIX), BF16),
            vmem((BLOCKS, SLOT_ALL, WIDE), F8),
            vmem((THIRDS, SLOT_ALL), F8),
            vmem((ROWS, 16, PIX), F32),
            vmem((ROWS, 16, PIX), F32),
            vmem((2, ROWS, 16, PIX), F32),
            vmem((2 * PIX, HALF), F32),
            dma((5,)),
            dma,
            dma,
            dma,
            dma,
            dma,
            dma,
            dma,
            dma,
            dma,
            dma,
            dma,
            dma,
            dma,
            dma((N_Z,)),
            dma,
            dma((N_Z,)),
        ],
        compiler_params=pltpu.CompilerParams(
            collective_id=0, has_side_effects=True, vmem_limit_bytes=56 * 1024 * 1024
        ),
    )(sky_map, tile_slot, pixel_offset, tile_list, noise_kernel)
    return result.reshape(TILES, PIX)


def solution(mesh):
    return jax.shard_map(
        on_device,
        mesh=mesh,
        in_specs=(
            P("det", None),
            P("det", "tm"),
            P("det", "tm"),
            P("det", "tm", None, None),
            P("det", None),
        ),
        out_specs=P("det", None),
        check_vma=False,
    )
```
